256 devices in a mesh: row: 16 (over y_hi, x, core), col: 8 (over z), rep: 2 (over y_lo).
Axes of the slice: x: 4, y: 4 (y_hi: 2, y_lo: 2; y = y_hi * 2 + y_lo), z: 8, core: 2. Of those that a mesh axis runs over, the one named last changes fastest.
Arguments:
- features: bfloat16 [32768, 512], P(('row', 'col', 'rep')), may hold values from -6 to 6
- tile_values: bfloat16 [32768, 128, 128], P(('row', 'col', 'rep')), as said below
- tile_coords: int32 [32768, 2], P(('row', 'col', 'rep')), may hold values from 0 to 15, as said below
- tile_counts: int32 [256], P(('row', 'col', 'rep')), may hold values from 16 to 128, as said below
- weight: bfloat16 [512, 512], replicated, may hold values from -0.25 to 0.25
- cotangent: bfloat16 [32768, 512], P(('row', 'col', 'rep')), may hold values from -6 to 6
Outputs:
- activations: bfloat16 [32768, 512], P(('row', 'col', 'rep'))
- grad_features: bfloat16 [32768, 512], P(('row', 'col', 'rep'))
- grad_weight: float32 [512, 512], replicated
The draws below stay inside these ranges and needn't reach their ends.
Inputs may be any that keep to these rules, and one draw needn't show every extreme that they name: `tile_values`: nonnegative edge weights; slots past a block's live count hold values that must be ignored. `tile_coords`: column 0 is a tile row below 16, column 1 a tile column below 16; within one block no tile position appears twice. `tile_counts`: live slots differ from block to block; some block uses all 128 slots.
All inputs are finite; a program needn't handle non-finite values.
Results may differ from the reference program's by a relative error of at most 0.028.
Values may be sent and summed in bfloat16 or wider, within the bound.
No kernel may reach another device: no remote copies, remote signals or barrier semaphores. Data moves between devices by JAX's collectives and lax.ppermute only.
A program may use at most 128 MiB of HBM per device.

```python
import math
import jax
import jax.numpy as jnp
from jax import lax

F = 512
TILE = 128
ROWS_DEV = 128
ROW_GROUPS = 16
COLUMN_GROUPS = 16
NODES = 32768
TILE_ROWS = 16
TILE_COLS = 16
TILES_DEV = 128
SLOTS = 32768


def draw_tile_values(key, part):
    key = jax.random.fold_in(key, 11)
    key_keep, key_vals = jax.random.split(key)
    shape_all = (SLOTS, TILE, TILE)
    norm_factor = 1.0 / math.sqrt(0.15 * COLUMN_GROUPS * TILE_COLS * TILE)
    keep = jax.random.bernoulli(key_keep, 0.5, shape_all).astype(jnp.float32)
    values_out = jax.random.uniform(key_vals, shape_all, jnp.float32, 0.5, 1.5)
    return (keep * values_out * norm_factor).astype(jnp.bfloat16)


def draw_tile_coords(key, part):
    key = jax.random.fold_in(key, 22)
    block_keys = jax.random.split(key, SLOTS // TILES_DEV)

    def one_block(block_key):
        chosen = jax.random.permutation(block_key, TILE_ROWS * TILE_COLS)[:TILES_DEV]
        return jnp.stack([chosen // TILE_COLS, chosen % TILE_COLS], axis=-1)
    return jax.vmap(one_block)(block_keys).reshape(SLOTS, 2).astype(jnp.int32)


def draw_tile_counts(key, part):
    key = jax.random.fold_in(key, 33)
    key_level, key_order = jax.random.split(key)
    block_total = SLOTS // TILES_DEV
    levels = jax.random.randint(key_level, (block_total,), 0, 64)
    order = jax.random.permutation(key_order, block_total)
    levels = levels.at[order[0]].set(63).at[order[1]].set(0)
    lowest = max(1, TILES_DEV // 8)
    return (lowest + (TILES_DEV - lowest) * levels // 63).astype(jnp.int32)


def block_levels(stream_key, shape, cuts, least, largest):
    level = 1.0
    for dim, blocks in cuts:
        draws = jax.random.uniform(jax.random.fold_in(jax.random.fold_in(stream_key, 6), dim), (blocks,), jnp.float32, least / len(cuts), largest / len(cuts))
        level = level * jnp.repeat(jnp.exp(draws), shape[dim] // blocks).reshape((-1,) + (1,) * (len(shape) - 1 - dim))
    return level


def gaussian(stream_key, dims, width, reach, cuts=(), held_as=jnp.bfloat16):
    drawn = width * jax.random.normal(stream_key, dims, jnp.float32)
    if cuts:
        drawn = drawn * block_levels(stream_key, dims, cuts, -0.22, 0.18)
    return jnp.clip(drawn, -reach, reach).astype(held_as)


def setup_inputs(seed: int = 0) -> dict:
    streams_of = jax.random.split(jax.random.key(seed), 7)
    return {
        "features": gaussian(streams_of[0], (NODES, F), 1.0, 6.0, ((0, 256),)),
        "tile_values": draw_tile_values(jax.random.fold_in(streams_of[6], 71), 0),
        "tile_coords": draw_tile_coords(jax.random.fold_in(streams_of[6], 71), 0),
        "tile_counts": draw_tile_counts(jax.random.fold_in(streams_of[6], 71), 0),
        "weight": gaussian(streams_of[4], (F, F), F ** -0.5, 0.25),
        "cotangent": gaussian(streams_of[5], (NODES, F), 1.0, 6.0, ((0, 256),)),
    }


def silu_slope(values_in):
    sigmoid_v = jax.nn.sigmoid(values_in)
    return sigmoid_v * (1.0 + values_in * (1.0 - sigmoid_v))

def reference(features, tile_values, tile_coords, tile_counts, weight, cotangent):
    feat_width = features.shape[1]
    block_total = ROW_GROUPS * COLUMN_GROUPS
    column_panels = features.reshape(ROW_GROUPS, COLUMN_GROUPS, ROWS_DEV, feat_width)
    column_panels = column_panels.transpose(1, 0, 2, 3).reshape(COLUMN_GROUPS, TILE_COLS, TILE, feat_width)
    slot_index = jnp.arange(TILES_DEV, dtype=jnp.int32)

    def device_tiles(device):
        begin = (device * TILES_DEV).astype(jnp.int32)
        tile_block = lax.dynamic_slice_in_dim(tile_values, begin, TILES_DEV, 0).astype(jnp.float32)
        coord_block = lax.dynamic_slice_in_dim(tile_coords, begin, TILES_DEV, 0)
        live_mask = (slot_index < tile_counts[device]).astype(jnp.float32)
        return (tile_block * live_mask[:, None, None], coord_block)

    def forward_block(device):
        tile_block, coord_block = device_tiles(device)
        source = column_panels[device % COLUMN_GROUPS]
        picked = source[coord_block[:, 1]].astype(jnp.float32)
        products = jnp.einsum('kij,kjf->kif', tile_block, picked)
        running = jnp.zeros((TILE_ROWS, TILE, feat_width), jnp.float32).at[coord_block[:, 0]].add(products)
        return running.astype(jnp.bfloat16)
    devices_all = jnp.arange(block_total, dtype=jnp.int32)
    partial_rows = lax.map(forward_block, devices_all)
    partial_rows = partial_rows.astype(jnp.float32).reshape(ROW_GROUPS, COLUMN_GROUPS, COLUMN_GROUPS * ROWS_DEV, feat_width)
    aggregated = lax.optimization_barrier(jnp.sum(partial_rows, axis=1)).reshape(NODES, feat_width).astype(jnp.bfloat16)
    pre_act = jnp.dot(aggregated, weight, preferred_element_type=jnp.float32)
    activations = jax.nn.silu(pre_act).astype(jnp.bfloat16)
    pre_grad = (cotangent.astype(jnp.float32) * silu_slope(pre_act)).astype(jnp.bfloat16)
    norm_factor = lax.rsqrt(jnp.float32(NODES))
    grad_weight = jnp.dot(aggregated.T, pre_grad, preferred_element_type=jnp.float32) * norm_factor
    row_grad = jnp.dot(pre_grad, weight.T, preferred_element_type=jnp.float32).astype(jnp.bfloat16)
    grad_panels = row_grad.reshape(ROW_GROUPS, TILE_ROWS, TILE, feat_width)

    def backward_block(device):
        tile_block, coord_block = device_tiles(device)
        source = grad_panels[device // COLUMN_GROUPS]
        picked = source[coord_block[:, 0]].astype(jnp.float32)
        products = jnp.einsum('kji,kjf->kif', tile_block, picked)
        running = jnp.zeros((TILE_COLS, TILE, feat_width), jnp.float32).at[coord_block[:, 1]].add(products)
        return running.astype(jnp.bfloat16)
    column_part = lax.map(backward_block, devices_all)
    column_part = column_part.astype(jnp.float32).reshape(ROW_GROUPS, COLUMN_GROUPS, ROW_GROUPS * ROWS_DEV, feat_width)
    summed = lax.optimization_barrier(jnp.sum(column_part, axis=0)).reshape(COLUMN_GROUPS, ROW_GROUPS, ROWS_DEV, feat_width)
    grad_features = summed.transpose(1, 0, 2, 3).reshape(NODES, feat_width).astype(jnp.bfloat16)
    return (activations, grad_features, grad_weight)
```

```python
import jax
import jax.numpy as jnp
from jax import lax
from jax.experimental import pallas as pl
from jax.experimental.pallas import tpu as pltpu
from jax.sharding import PartitionSpec as P

TILE = 128
BUNCH = 16
F32 = jnp.float32
BF16 = jnp.bfloat16
MIB = 1024 * 1024


def wide_sum(*terms):
    total = terms[0].astype(F32)
    for term in terms[1:]:
        total = total + term.astype(F32)
    return total.astype(BF16)


def dense_kernel(flip, counts_ref, places_ref, tiles_ref, dense_ref):
    step = pl.program_id(0)

    @pl.when(step == 0)
    def _():
        dense_ref[...] = jnp.zeros_like(dense_ref)

    def place(j, carry):
        slot = step * BUNCH + j

        @pl.when(slot < counts_ref[0])
        def _():
            top = pl.multiple_of(places_ref[2 * slot] * TILE, TILE)
            left = pl.multiple_of(places_ref[2 * slot + 1] * TILE, TILE)
            tile = tiles_ref[j]
            if flip:
                dense_ref[pl.ds(left, TILE), pl.ds(top, TILE)] = tile.T
            else:
                dense_ref[pl.ds(top, TILE), pl.ds(left, TILE)] = tile

        return carry

    lax.fori_loop(0, BUNCH, place, 0)


def dense_block(tile_values, places, tile_counts, side, flip):
    slots = tile_values.shape[0]
    return pl.pallas_call(
        lambda *refs: dense_kernel(flip, *refs),
        out_shape=jax.ShapeDtypeStruct((side, side), BF16),
        grid_spec=pltpu.PrefetchScalarGridSpec(
            num_scalar_prefetch=2,
            grid=(slots // BUNCH,),
            in_specs=[pl.BlockSpec((BUNCH, TILE, TILE), lambda g, *_: (g, 0, 0))],
            out_specs=pl.BlockSpec((side, side), lambda g, *_: (0, 0)),
        ),
        compiler_params=pltpu.CompilerParams(vmem_limit_bytes=28 * MIB),
        cost_estimate=pl.CostEstimate(flops=0, bytes_accessed=12 * MIB, transcendentals=0),
        name="flipped_build" if flip else "dense_build",
    )(tile_counts, places.reshape(-1), tile_values)


def pieces_dot_kernel(starts, dense_ref, *refs):
    out_ref = refs[-1]
    total = None
    for start, piece in zip(starts, refs[:-1]):
        depth = piece.shape[0]
        term = jnp.dot(
            dense_ref[:, start : start + depth], piece[...], preferred_element_type=F32
        )
        total = term if total is None else total + term
    out_ref[...] = total.astype(BF16)


def pieces_dot(dense, pieces, starts, first, rows, name):
    block = 256
    side = dense.shape[1]
    width = pieces[0].shape[1]
    return pl.pallas_call(
        lambda *refs: pieces_dot_kernel(starts, *refs),
        out_shape=jax.ShapeDtypeStruct((rows, width), BF16),
        grid=(rows // block,),
        in_specs=[pl.BlockSpec((block, side), lambda g: (g + first // block, 0))]
        + [pl.BlockSpec(p.shape, lambda g: (0, 0)) for p in pieces],
        out_specs=pl.BlockSpec((block, width), lambda g: (g, 0)),
        compiler_params=pltpu.CompilerParams(vmem_limit_bytes=28 * MIB),
        cost_estimate=pl.CostEstimate(
            flops=2 * rows * side * width, bytes_accessed=2 * rows * side, transcendentals=0
        ),
        name=name,
    )(dense, *pieces)


def layer_kernel(agg_ref, weight_ref, cot_ref, act_ref, pre_grad_ref, row_grad_ref):
    pre_act = jnp.dot(agg_ref[...], weight_ref[...], preferred_element_type=F32)
    gate = 1.0 / (1.0 + jnp.exp(-pre_act))
    act_ref[...] = (pre_act * gate).astype(BF16)
    slope = gate * (1.0 + pre_act * (1.0 - gate))
    pre_grad = (cot_ref[...].astype(F32) * slope).astype(BF16)
    pre_grad_ref[...] = pre_grad
    row_grad_ref[...] = lax.dot_general(
        pre_grad, weight_ref[...], (((1,), (1,)), ((), ())), preferred_element_type=F32
    ).astype(BF16)


def layer(aggregated, weight, cotangent):
    shape = jax.ShapeDtypeStruct(aggregated.shape, BF16)
    return pl.pallas_call(
        layer_kernel, out_shape=(shape, shape, shape), name="layer"
    )(aggregated, weight, cotangent)


def swap_core(value):
    return lax.ppermute(value, "row", [(r, r ^ 1) for r in range(16)])


def swap_half(value):
    return lax.ppermute(value, "row", [(r, r ^ 8) for r in range(16)])


def along_x(value, ahead):
    perm = []
    for r in range(16):
        half, x, core = r >> 3, (r >> 1) & 3, r & 1
        step = 1 if (core == 0) == ahead else -1
        perm.append((r, half * 8 + ((x + step) % 4) * 2 + core))
    return lax.ppermute(value, "row", perm)


def along_z(value, step):
    return lax.ppermute(value, "col", [(z, (z + step) % 8) for z in range(8)])


def swap_rep(value):
    return lax.ppermute(value, "rep", [(0, 1), (1, 0)])


def column_places(tile_columns):
    me = lax.axis_index("row")
    half, x, core = me >> 3, (me >> 1) & 3, me & 1
    dy = (tile_columns >> 3) ^ half
    dc = (tile_columns & 1) ^ core
    dx = (((tile_columns >> 1) & 3) - x) & 3
    e = jnp.where(core == 0, dx, (-dx) & 3)
    base = jnp.where(
        e == 0,
        2 * dc,
        jnp.where(e == 3, 4 + 2 * dc, jnp.where(e == 1, 10 + 2 * (1 - dc), 8 + 6 * dc)),
    )
    return base + dy


def row_places(tile_rows):
    z, low = lax.axis_index("col"), lax.axis_index("rep")
    dz = ((tile_rows >> 1) - z) & 7
    return 2 * dz + ((tile_rows & 1) ^ low)


def gather_row(own):
    pair = jnp.concatenate([own, swap_half(own)], 0)
    other = swap_core(pair)
    chip = jnp.concatenate([pair, other], 0)
    side = along_x(chip, True)
    far = along_x(side[:256], True)
    side_other = swap_core(side)
    far_other = swap_core(far)
    return (chip, side, far, side_other, far_other), (0, 512, 1024, 1280, 1792)


def scatter_row(part):
    far_other = swap_core(part[1792:2048])
    side_other = swap_core(part[1280:1792])
    far = along_x(wide_sum(part[1024:1280], far_other), False)
    side = jnp.concatenate(
        [wide_sum(part[512:768], side_other[:256], far), wide_sum(part[768:1024], side_other[256:])], 0
    )
    chip = along_x(side, False)
    mine = part[:256].astype(F32) + chip[:256].astype(F32)
    theirs = swap_core(wide_sum(part[256:512], chip[256:]))
    kept = swap_half(wide_sum(mine[128:], theirs[128:]))
    return wide_sum(mine[:128], theirs[:128], kept)


def scatter_col(block_of):
    middle = block_of(4)
    up = along_z(middle[:128], 1)
    down = along_z(middle[128:], -1)
    for d in (3, 2, 1):
        ahead, behind = block_of(d), block_of(8 - d)
        if d == 3:
            up_sum = jnp.concatenate([wide_sum(ahead[:128], up), ahead[128:]], 0)
            down_sum = jnp.concatenate([behind[:128], wide_sum(behind[128:], down)], 0)
        else:
            up_sum, down_sum = wide_sum(ahead, up), wide_sum(behind, down)
        up, down = along_z(up_sum, 1), along_z(down_sum, -1)
    here = block_of(0)
    theirs = swap_rep(wide_sum(here[128:], up[128:], down[128:]))
    return wide_sum(here[:128], up[:128], down[:128], theirs)


def gather_col(own):
    here = jnp.concatenate([own, swap_rep(own)], 0)
    from_up, from_down = [here], [here]
    for step in range(3):
        from_down.append(along_z(from_down[-1], 1))
        from_up.append(along_z(from_up[-1], -1))
    far_down = along_z(from_down[3][:128], 1)
    far_up = along_z(from_up[3][128:], -1)
    pieces = (here, from_up[1], from_up[2], from_up[3], far_down, far_up)
    pieces += (from_down[3], from_down[2], from_down[1])
    return pieces, (0, 256, 512, 768, 1024, 1152, 1280, 1536, 1792)


def keep_half(total, bit, swap):
    rows = total.shape[0] // 2
    kept = lax.dynamic_slice_in_dim(total, bit * rows, rows, 0)
    sent = lax.dynamic_slice_in_dim(total, (1 - bit) * rows, rows, 0).astype(BF16)
    return kept + swap(sent).astype(F32)


def swap_row(value, mask):
    return lax.ppermute(value, "row", [(r, r ^ mask) for r in range(16)])


def swap_z(value, mask):
    return lax.ppermute(value, "col", [(z, z ^ mask) for z in range(8)])


def join_halves(mine, bit, swap):
    theirs = swap(mine)
    low = jnp.where(bit == 0, mine, theirs)
    high = jnp.where(bit == 0, theirs, mine)
    return jnp.concatenate([low, high], 0)


ROW_MASKS = (1, 2, 4, 8)


def weight_share(local):
    me = lax.axis_index("row")
    for mask in ROW_MASKS:
        bit = (me // mask) & 1
        local = keep_half(local, bit, lambda v, mask=mask: swap_row(v, mask))
    share = local.astype(BF16)
    share = wide_sum(share, swap_rep(share))
    for mask in (1, 2, 4):
        share = wide_sum(share, swap_z(share, mask))
    return share


def weight_whole(share):
    me = lax.axis_index("row")
    for mask in ROW_MASKS[::-1]:
        bit = (me // mask) & 1
        share = join_halves(share, bit, lambda v, mask=mask: swap_row(v, mask))
    return share.astype(F32)


def body(features, tile_values, tile_coords, tile_counts, weight, cotangent):
    nodes = features.shape[0] * 256
    places = jnp.stack([row_places(tile_coords[:, 0]), column_places(tile_coords[:, 1])], -1)
    side = 2048
    dense = dense_block(tile_values, places, tile_counts, side, False)
    flipped = dense_block(tile_values, places, tile_counts, side, True)
    panel, starts = gather_row(features)
    first = pieces_dot(dense, panel, starts, 1024, 256, "rows_far")
    rest_high = pieces_dot(dense, panel, starts, 1280, 768, "rows_behind")
    rest_low = pieces_dot(dense, panel, starts, 0, 1024, "rows_ahead")

    def block_of(d):
        if d == 4:
            return first
        if d > 4:
            return rest_high[256 * (d - 5) : 256 * (d - 4)]
        return rest_low[256 * d : 256 * (d + 1)]

    aggregated = scatter_col(block_of)
    activations, pre_grad, own_grad = layer(aggregated, weight, cotangent)
    row_grad, depths = gather_col(own_grad)
    weight_local = lax.dot_general(
        aggregated, pre_grad, (((0,), (0,)), ((), ())), preferred_element_type=F32
    )
    grad_weight = weight_whole(weight_share(weight_local)) * lax.rsqrt(F32(nodes))
    column_part = pieces_dot(flipped, row_grad, depths, 0, side, "columns")
    grad_features = scatter_row(column_part)
    return (activations, grad_features, grad_weight)


def solution(mesh):
    split = ("row", "col", "rep")
    placed = (P(split, None), P(split, None, None), P(split, None), P(split), P(), P(split, None))
    return jax.shard_map(
        body,
        mesh=mesh,
        in_specs=placed,
        out_specs=(P(split, None), P(split, None), P()),
        check_vma=False,
    )
```

```python
import jax
import jax.numpy as jnp
from jax import lax
from jax.experimental import pallas as pl
from jax.experimental.pallas import tpu as pltpu
from jax.sharding import PartitionSpec as P

TILE = 128
BUNCH = 16
SIDE = 2048
BLOCK = 256
F32 = jnp.float32
BF16 = jnp.bfloat16
MIB = 1024 * 1024
SCOPED = 8 * MIB
WHOLE = pl.BlockSpec(memory_space=pltpu.VMEM)


def wide_sum(*terms):
    total = terms[0].astype(F32)
    for term in terms[1:]:
        total = total + term.astype(F32)
    return total.astype(BF16)


def fence(*values):
    return lax.optimization_barrier(values)


def stack(*values):
    return jnp.concatenate(values, 0)


def dense_kernel(counts_ref, places_ref, tiles_ref, dense_ref, held_ref, arrived):
    bunches = held_ref.shape[0] // BUNCH

    def fetch(b):
        part = pl.ds(b * BUNCH, BUNCH)
        return pltpu.make_async_copy(tiles_ref.at[part], held_ref.at[part], arrived.at[b])

    for b in range(bunches):
        fetch(b).start()
    dense_ref[...] = jnp.zeros_like(dense_ref)
    live = counts_ref[0]
    for b in range(bunches):
        fetch(b).wait()

        def place(j, carry, b=b):
            slot = b * BUNCH + j

            @pl.when(slot < live)
            def _():
                top = pl.multiple_of(places_ref[2 * slot] * TILE, TILE)
                left = pl.multiple_of(places_ref[2 * slot + 1] * TILE, TILE)
                dense_ref[pl.ds(top, TILE), pl.ds(left, TILE)] = held_ref[slot]

            return carry

        lax.fori_loop(0, BUNCH, place, 0)


def dense_block(tile_values, places, tile_counts):
    slots = tile_values.shape[0]
    smem = pl.BlockSpec(memory_space=pltpu.SMEM)
    return pl.pallas_call(
        dense_kernel,
        out_shape=jax.ShapeDtypeStruct((SIDE, SIDE), BF16),
        in_specs=[smem, smem, pl.BlockSpec(memory_space=pltpu.HBM)],
        out_specs=WHOLE,
        scratch_shapes=[
            pltpu.VMEM(tile_values.shape, BF16),
            pltpu.SemaphoreType.DMA((slots // BUNCH,)),
        ],
        compiler_params=pltpu.CompilerParams(vmem_limit_bytes=SCOPED),
        cost_estimate=pl.CostEstimate(flops=0, bytes_accessed=12 * MIB, transcendentals=0),
        name="dense_build",
    )(tile_counts, places, tile_values)


def rows_kernel(first, dense_ref, *refs):
    pieces, (out_ref, panel_ref) = refs[:-2], refs[-2:]
    at = 0
    for piece in pieces:
        panel_ref[at : at + piece.shape[0], :] = piece[...]
        at += piece.shape[0]
    for begin in range(0, out_ref.shape[0], BLOCK):
        out_ref[begin : begin + BLOCK, :] = jnp.dot(
            dense_ref[pl.ds((first + begin) % SIDE, BLOCK), :],
            panel_ref[...],
            preferred_element_type=F32,
        ).astype(BF16)


def rows_dot(dense, pieces, first, rows, name):
    width = pieces[0].shape[1]
    return pl.pallas_call(
        lambda *refs: rows_kernel(first, *refs),
        out_shape=jax.ShapeDtypeStruct((rows, width), BF16),
        in_specs=[WHOLE] * (1 + len(pieces)),
        out_specs=WHOLE,
        scratch_shapes=[pltpu.VMEM((SIDE, width), BF16)],
        compiler_params=pltpu.CompilerParams(vmem_limit_bytes=SCOPED),
        cost_estimate=pl.CostEstimate(
            flops=2 * rows * SIDE * width, bytes_accessed=2 * rows * SIDE, transcendentals=0
        ),
        name=name,
    )(dense, *pieces)


def columns_kernel(first, dense_ref, *refs):
    pieces, (out_ref, panel_ref) = refs[:-2], refs[-2:]
    width = panel_ref.shape[0]
    down, across = 0, 0
    for piece in pieces:
        depth, step = piece.shape
        panel_ref[down : down + depth, across : across + step] = piece[...]
        down += depth
        if down == width:
            down, across = 0, across + step
    for block in range(0, out_ref.shape[0], 2):
        begin = first + block * TILE
        product = jnp.dot(
            panel_ref[...], dense_ref[:, begin : begin + BLOCK], preferred_element_type=F32
        ).astype(BF16)
        out_ref[block] = product[:, :TILE]
        out_ref[block + 1] = product[:, TILE:]


def columns_dot(dense, pieces, first, blocks, name):
    width = pieces[0].shape[0]
    return pl.pallas_call(
        lambda *refs: columns_kernel(first, *refs),
        out_shape=jax.ShapeDtypeStruct((blocks, width, TILE), BF16),
        in_specs=[WHOLE] * (1 + len(pieces)),
        out_specs=WHOLE,
        scratch_shapes=[pltpu.VMEM((width, SIDE), BF16)],
        compiler_params=pltpu.CompilerParams(vmem_limit_bytes=SCOPED),
        cost_estimate=pl.CostEstimate(
            flops=2 * blocks * TILE * SIDE * width,
            bytes_accessed=2 * blocks * TILE * SIDE,
            transcendentals=0,
        ),
        name=name,
    )(dense, *pieces)


def layer_kernel(mine_ref, theirs_ref, weight_ref, cot_ref, twin_ref, agg_ref, act_ref, pre_grad_ref, grad_ref):
    half = cot_ref.shape[0]
    for at, cot in ((0, cot_ref), (half, twin_ref)):
        rows = slice(at, at + half)
        total = mine_ref[rows, :].astype(F32) + theirs_ref[half - at : 2 * half - at, :].astype(F32)
        aggregated = total.astype(BF16)
        agg_ref[rows, :] = aggregated
        pre_act = jnp.dot(aggregated, weight_ref[...], preferred_element_type=F32)
        gate = 1.0 / (1.0 + jnp.exp(-pre_act))
        if at == 0:
            act_ref[...] = (pre_act * gate).astype(BF16)
        slope = gate * (1.0 + pre_act * (1.0 - gate))
        pre_grad = (cot[...].astype(F32) * slope).astype(BF16)
        pre_grad_ref[rows, :] = pre_grad
        grad_ref[:, rows] = lax.dot_general(
            weight_ref[...], pre_grad, (((1,), (1,)), ((), ())), preferred_element_type=F32
        ).astype(BF16)


def layer(mine, theirs, weight, cotangent, cot_twin):
    rows, width = cotangent.shape
    both = jax.ShapeDtypeStruct((2 * rows, width), BF16)
    own = jax.ShapeDtypeStruct((rows, width), BF16)
    turned = jax.ShapeDtypeStruct((width, 2 * rows), BF16)
    return pl.pallas_call(
        layer_kernel,
        out_shape=(both, own, both, turned),
        in_specs=[WHOLE] * 5,
        out_specs=(WHOLE,) * 4,
        compiler_params=pltpu.CompilerParams(vmem_limit_bytes=SCOPED),
        name="layer",
    )(mine, theirs, weight, cotangent, cot_twin)


def finish_kernel(*refs):
    total = refs[0][...].astype(F32)
    for part in refs[1:-1]:
        total = total + part[...].astype(F32)
    refs[-1][...] = total.T.astype(BF16)


def finish(*parts):
    width, rows = parts[0].shape
    return pl.pallas_call(
        finish_kernel,
        out_shape=jax.ShapeDtypeStruct((rows, width), BF16),
        in_specs=[WHOLE] * len(parts),
        out_specs=WHOLE,
        compiler_params=pltpu.CompilerParams(vmem_limit_bytes=SCOPED),
        name="finish",
    )(*parts)


def weight_part_kernel(where_ref, agg_ref, pre_grad_ref, kept_ref, sent_ref):
    low, core = where_ref[0], where_ref[1]

    def rows_of(which):
        at = pl.multiple_of(low * 256 + which * 128, 128)
        return lax.dot_general(
            agg_ref[:, pl.ds(at, 128)],
            pre_grad_ref[...],
            (((0,), (0,)), ((), ())),
            preferred_element_type=F32,
        )

    kept_ref[...] = rows_of(core)
    sent_ref[...] = rows_of(1 - core).astype(BF16)


def weight_part(where, aggregated, pre_grad):
    width = pre_grad.shape[1]
    return pl.pallas_call(
        weight_part_kernel,
        out_shape=(
            jax.ShapeDtypeStruct((128, width), F32),
            jax.ShapeDtypeStruct((128, width), BF16),
        ),
        in_specs=[pl.BlockSpec(memory_space=pltpu.SMEM)] + [WHOLE] * 2,
        out_specs=(WHOLE,) * 2,
        compiler_params=pltpu.CompilerParams(vmem_limit_bytes=SCOPED),
        name="weight_part",
    )(where, aggregated, pre_grad)


def weight_place_kernel(norm, where_ref, own_ref, core_ref, rep_ref, both_ref, out_ref):
    low, core = where_ref[0], where_ref[1]
    rows = own_ref.shape[0]
    for value, at_low, at_core in (
        (own_ref, low, core),
        (core_ref, low, 1 - core),
        (rep_ref, 1 - low, core),
        (both_ref, 1 - low, 1 - core),
    ):
        at = pl.multiple_of((at_low * 2 + at_core) * rows, rows)
        out_ref[pl.ds(at, rows), :] = value[...].astype(F32) * norm


def weight_place(where, blocks, norm):
    rows, width = blocks[0].shape
    return pl.pallas_call(
        lambda *refs: weight_place_kernel(norm, *refs),
        out_shape=jax.ShapeDtypeStruct((4 * rows, width), F32),
        in_specs=[pl.BlockSpec(memory_space=pltpu.SMEM)] + [WHOLE] * 4,
        out_specs=WHOLE,
        compiler_params=pltpu.CompilerParams(vmem_limit_bytes=SCOPED),
        name="weight_place",
    )(where, *blocks)


def swap_row(value, mask):
    return lax.ppermute(value, "row", [(r, r ^ mask) for r in range(16)])


def swap_core(value):
    return swap_row(value, 1)


def along_x(value, step):
    def target(r):
        return (r & 9) | ((((r >> 1) + step) & 3) << 1)

    return lax.ppermute(value, "row", [(r, target(r)) for r in range(16)])


def along_z(value, step):
    return lax.ppermute(value, "col", [(z, (z + step) % 8) for z in range(8)])


def swap_z(value, mask):
    return lax.ppermute(value, "col", [(z, z ^ mask) for z in range(8)])


def swap_rep(value):
    return lax.ppermute(value, "rep", [(0, 1), (1, 0)])


def swap_core_rep(value):
    pairs = [(2 * r + low, 2 * (r ^ 1) + 1 - low) for r in range(16) for low in range(2)]
    return lax.ppermute(value, ("row", "rep"), pairs)


LATE = ((1, 1), (3, 1), (2, 0), (2, 1))
SOON = ((0, 1), (1, 0), (3, 0))
ORDER = [(x, y, 1) for x, y in LATE] + [(x, y, 0) for x, y in LATE]
ORDER += [(x, y, 1) for x, y in SOON] + [(x, y, 0) for x, y in SOON]
ORDER += [(0, 0, 1), (0, 0, 0)]


def column_places(tile_columns):
    me = lax.axis_index("row")
    half, x, core = me >> 3, (me >> 1) & 3, me & 1
    dy = (tile_columns >> 3) ^ half
    dx = (((tile_columns >> 1) & 3) - x) & 3
    dc = (tile_columns & 1) ^ core
    key = dx * 4 + dy * 2 + dc
    place = jnp.zeros_like(key)
    for at, (bx, by, bc) in enumerate(ORDER):
        place = jnp.where(key == bx * 4 + by * 2 + bc, at, place)
    return place


def row_places(tile_rows):
    z, low = lax.axis_index("col"), lax.axis_index("rep")
    dz = ((tile_rows >> 1) - z) & 7
    return 2 * dz + ((tile_rows & 1) ^ low)


def body(features, tile_values, tile_coords, tile_counts, weight, cotangent):
    nodes = features.shape[0] * 256
    where = jnp.stack([lax.axis_index("rep"), lax.axis_index("row") & 1]).astype(jnp.int32)
    places = jnp.stack([row_places(tile_coords[:, 0]), column_places(tile_coords[:, 1])], -1)
    places = places.reshape(-1)

    half = swap_row(features, 8)
    left = along_x(features, 1)
    right = along_x(features, -1)
    core = swap_core(features)
    half, left, right, core, places, where = fence(half, left, right, core, places, where)
    sides = swap_row(stack(right, left), 8)
    far_half = swap_row(half, 4)
    far = along_x(left, 1)
    core_soon = swap_core(stack(half, right, left))
    dense = dense_block(tile_values, places, tile_counts)
    sides, far, far_half, core_soon, dense = fence(sides, far, far_half, core_soon, dense)
    late = stack(sides, far, far_half)
    core_late = swap_core(late)
    cot_twin = swap_rep(cotangent)
    pieces = (core_late, late, core_soon, half, right, left, core, features)

    middle = rows_dot(dense, pieces, 1024, 256, "rows_middle")
    up, down, middle = fence(middle[:128], middle[128:], middle)
    up, down = along_z(up, 1), along_z(down, -1)
    rest = rows_dot(dense, pieces, 1280, 1792, "rows_rest")

    def block(d):
        at = (d - 5) % 8 * 256
        return rest[at : at + 256]

    ahead, behind = block(3), block(5)
    up = stack(wide_sum(ahead[:128], up), ahead[128:])
    down = stack(behind[:128], wide_sum(behind[128:], down))
    up, down, cot_twin = fence(up, down, cot_twin)
    up, down = along_z(up, 1), along_z(down, -1)
    up, down = fence(up, down)
    up, down = fence(wide_sum(block(2), up), wide_sum(block(6), down))
    up, down = along_z(up, 1), along_z(down, -1)
    up, down = fence(up, down)
    up, down = fence(wide_sum(block(1), up), wide_sum(block(7), down))
    up, down = along_z(up, 1), along_z(down, -1)
    mine = wide_sum(block(0), up, down)
    theirs = swap_rep(mine)
    aggregated, activations, pre_grad, here = layer(mine, theirs, weight, cotangent, cot_twin)

    here, aggregated, pre_grad = fence(here, aggregated, pre_grad)
    below, above = along_z(here, 1), along_z(here, -1)
    kept, sent = weight_part(where, aggregated, pre_grad)
    taken = swap_core(sent)
    near = below, above

    below, above, taken = fence(below, above, taken)
    share = wide_sum(kept, taken)
    below, above, share = fence(below, above, share)
    below, above = along_z(below, 1), along_z(above, -1)
    taken = [swap_row(share, 2 * m) for m in (1, 2, 3)]
    next_near = below, above

    below, above, *taken = fence(below, above, *taken)
    share = (share.astype(F32) + taken[0].astype(F32)) + (taken[1].astype(F32) + taken[2].astype(F32))
    share = share.astype(BF16)
    below, above, share = fence(below, above, share)
    below, above = along_z(below, 1), along_z(above, -1)
    taken = swap_row(share, 8)
    far = below, above

    below, above, taken = fence(below, above, taken)
    share = wide_sum(share, taken)
    below, above, share = fence(below[:256], above[256:], share)
    below, above = along_z(below, 1), along_z(above, -1)
    taken = swap_z(share, 1)
    below, above, taken = fence(below, above, taken)
    share = wide_sum(share, taken)
    rows = (here, near[1], next_near[1], far[1], below, above, far[0], next_near[0], near[0])

    other = columns_dot(dense, rows, 0, 4, "columns_other")
    other, share = fence(other, share)
    other = swap_core(other)
    taken = swap_z(share, 2)
    rest = columns_dot(dense, rows, 512, 12, "columns_rest")
    other, rest, taken = fence(other, rest, taken)
    late = wide_sum(rest[:4], other)
    share = wide_sum(share, taken)
    late, soon, share = fence(late, rest[4:7], share)
    sides = swap_row(late[:2], 8)
    far_half = swap_row(late[3], 4)
    far = along_x(late[2], -1)
    soon = swap_core(soon)
    taken = swap_z(share, 4)

    sides, far_half, far, soon, taken = fence(sides, far_half, far, soon, taken)
    half = wide_sum(rest[7], soon[0], far_half)
    right = wide_sum(rest[8], soon[1], sides[0])
    left = wide_sum(rest[9], soon[2], sides[1], far)
    share = wide_sum(share, taken)
    half, right, left, core, share = fence(half, right, left, rest[10], share)
    half, right, left = swap_row(half, 8), along_x(right, 1), along_x(left, -1)
    core = swap_core(core)
    shares = share, swap_core(share), swap_rep(share), swap_core_rep(share)
    grad_weight = weight_place(where, shares, 1.0 / nodes**0.5)
    grad_features = finish(rest[11], half, right, left, core)
    return (activations, grad_features, grad_weight)


def solution(mesh):
    split = ("row", "col", "rep")
    placed = (P(split, None), P(split, None, None), P(split, None), P(split), P(), P(split, None))
    return jax.shard_map(
        body,
        mesh=mesh,
        in_specs=placed,
        out_specs=(P(split, None), P(split, None), P()),
        check_vma=False,
    )
```

```python
import jax
import jax.numpy as jnp
from jax import lax
from jax.experimental import pallas as pl
from jax.experimental.pallas import tpu as pltpu
from jax.sharding import PartitionSpec as P

TILE = 128
BUNCH = 16
SIDE = 2048
BLOCK = 256
F32 = jnp.float32
BF16 = jnp.bfloat16
MIB = 1024 * 1024
SCOPED = 8 * MIB
WHOLE = pl.BlockSpec(memory_space=pltpu.VMEM)


def wide_sum(*terms):
    total = terms[0].astype(F32)
    for term in terms[1:]:
        total = total + term.astype(F32)
    return total.astype(BF16)


def fence(*values):
    return lax.optimization_barrier(values)


def stack(*values):
    return jnp.concatenate(values, 0)


def dense_kernel(counts_ref, places_ref, tiles_ref, dense_ref, held_ref, arrived):
    bunches = held_ref.shape[0] // BUNCH

    def fetch(b):
        part = pl.ds(b * BUNCH, BUNCH)
        return pltpu.make_async_copy(tiles_ref.at[part], held_ref.at[part], arrived.at[b])

    for b in range(bunches):
        fetch(b).start()
    dense_ref[...] = jnp.zeros_like(dense_ref)
    live = counts_ref[0]
    for b in range(bunches):
        fetch(b).wait()

        def place(j, carry, b=b):
            slot = b * BUNCH + j

            @pl.when(slot < live)
            def _():
                top = pl.multiple_of(places_ref[2 * slot] * TILE, TILE)
                left = pl.multiple_of(places_ref[2 * slot + 1] * TILE, TILE)
                dense_ref[pl.ds(top, TILE), pl.ds(left, TILE)] = held_ref[slot]

            return carry

        lax.fori_loop(0, BUNCH, place, 0)


def dense_block(tile_values, places, tile_counts):
    slots = tile_values.shape[0]
    smem = pl.BlockSpec(memory_space=pltpu.SMEM)
    return pl.pallas_call(
        dense_kernel,
        out_shape=jax.ShapeDtypeStruct((SIDE, SIDE), BF16),
        in_specs=[smem, smem, pl.BlockSpec(memory_space=pltpu.HBM)],
        out_specs=WHOLE,
        scratch_shapes=[
            pltpu.VMEM(tile_values.shape, BF16),
            pltpu.SemaphoreType.DMA((slots // BUNCH,)),
        ],
        compiler_params=pltpu.CompilerParams(vmem_limit_bytes=SCOPED),
        cost_estimate=pl.CostEstimate(flops=0, bytes_accessed=12 * MIB, transcendentals=0),
        name="dense_build",
    )(tile_counts, places, tile_values)


def rows_kernel(starts, dense_ref, *refs):
    pieces, (out_ref, panel_ref) = refs[:-2], refs[-2:]
    at = 0
    for piece in pieces:
        panel_ref[at : at + piece.shape[0], :] = piece[...]
        at += piece.shape[0]
    for i, start in enumerate(starts):
        out_ref[i * BLOCK : (i + 1) * BLOCK, :] = jnp.dot(
            dense_ref[start : start + BLOCK, :], panel_ref[...], preferred_element_type=F32
        ).astype(BF16)


def rows_dot(dense, pieces, starts, name):
    width = pieces[0].shape[1]
    rows = BLOCK * len(starts)
    return pl.pallas_call(
        lambda *refs: rows_kernel(starts, *refs),
        out_shape=jax.ShapeDtypeStruct((rows, width), BF16),
        in_specs=[WHOLE] * (1 + len(pieces)),
        out_specs=WHOLE,
        scratch_shapes=[pltpu.VMEM((SIDE, width), BF16)],
        compiler_params=pltpu.CompilerParams(vmem_limit_bytes=SCOPED),
        cost_estimate=pl.CostEstimate(
            flops=2 * rows * SIDE * width, bytes_accessed=2 * rows * SIDE, transcendentals=0
        ),
        name=name,
    )(dense, *pieces)


def columns_kernel(first, dense_ref, *refs):
    pieces, (out_ref, panel_ref) = refs[:-2], refs[-2:]
    width = panel_ref.shape[0]
    down, across = 0, 0
    for piece in pieces:
        depth, step = piece.shape
        panel_ref[down : down + depth, across : across + step] = piece[...]
        down += depth
        if down == width:
            down, across = 0, across + step
    for block in range(0, out_ref.shape[0], 2):
        begin = first + block * TILE
        product = jnp.dot(
            panel_ref[...], dense_ref[:, begin : begin + BLOCK], preferred_element_type=F32
        ).astype(BF16)
        out_ref[block] = product[:, :TILE]
        out_ref[block + 1] = product[:, TILE:]


def columns_dot(dense, pieces, first, blocks, name):
    width = pieces[0].shape[0]
    return pl.pallas_call(
        lambda *refs: columns_kernel(first, *refs),
        out_shape=jax.ShapeDtypeStruct((blocks, width, TILE), BF16),
        in_specs=[WHOLE] * (1 + len(pieces)),
        out_specs=WHOLE,
        scratch_shapes=[pltpu.VMEM((width, SIDE), BF16)],
        compiler_params=pltpu.CompilerParams(vmem_limit_bytes=SCOPED),
        cost_estimate=pl.CostEstimate(
            flops=2 * blocks * TILE * SIDE * width,
            bytes_accessed=2 * blocks * TILE * SIDE,
            transcendentals=0,
        ),
        name=name,
    )(dense, *pieces)


def layer_kernel(mine_ref, theirs_ref, weight_ref, cot_ref, twin_ref, agg_ref, act_ref, pre_grad_ref, grad_ref):
    half = cot_ref.shape[0]
    for at, cot in ((0, cot_ref), (half, twin_ref)):
        rows = slice(at, at + half)
        total = mine_ref[rows, :].astype(F32) + theirs_ref[half - at : 2 * half - at, :].astype(F32)
        aggregated = total.astype(BF16)
        agg_ref[rows, :] = aggregated
        pre_act = jnp.dot(aggregated, weight_ref[...], preferred_element_type=F32)
        gate = 1.0 / (1.0 + jnp.exp(-pre_act))
        if at == 0:
            act_ref[...] = (pre_act * gate).astype(BF16)
        slope = gate * (1.0 + pre_act * (1.0 - gate))
        pre_grad = (cot[...].astype(F32) * slope).astype(BF16)
        pre_grad_ref[rows, :] = pre_grad
        grad_ref[:, rows] = lax.dot_general(
            weight_ref[...], pre_grad, (((1,), (1,)), ((), ())), preferred_element_type=F32
        ).astype(BF16)


def layer(mine, theirs, weight, cotangent, cot_twin):
    rows, width = cotangent.shape
    both = jax.ShapeDtypeStruct((2 * rows, width), BF16)
    own = jax.ShapeDtypeStruct((rows, width), BF16)
    turned = jax.ShapeDtypeStruct((width, 2 * rows), BF16)
    return pl.pallas_call(
        layer_kernel,
        out_shape=(both, own, both, turned),
        in_specs=[WHOLE] * 5,
        out_specs=(WHOLE,) * 4,
        compiler_params=pltpu.CompilerParams(vmem_limit_bytes=SCOPED),
        name="layer",
    )(mine, theirs, weight, cotangent, cot_twin)


def finish_kernel(*refs):
    total = refs[0][...].astype(F32)
    for part in refs[1:-1]:
        total = total + part[...].astype(F32)
    refs[-1][...] = total.T.astype(BF16)


def finish(*parts):
    width, rows = parts[0].shape
    return pl.pallas_call(
        finish_kernel,
        out_shape=jax.ShapeDtypeStruct((rows, width), BF16),
        in_specs=[WHOLE] * len(parts),
        out_specs=WHOLE,
        compiler_params=pltpu.CompilerParams(vmem_limit_bytes=SCOPED),
        name="finish",
    )(*parts)


def weight_part_kernel(where_ref, agg_ref, pre_grad_ref, kept_ref, sent_ref):
    low, core = where_ref[0], where_ref[1]

    def rows_of(which):
        at = pl.multiple_of(low * 256 + which * 128, 128)
        return lax.dot_general(
            agg_ref[:, pl.ds(at, 128)],
            pre_grad_ref[...],
            (((0,), (0,)), ((), ())),
            preferred_element_type=F32,
        )

    kept_ref[...] = rows_of(core)
    sent_ref[...] = rows_of(1 - core).astype(BF16)


def weight_part(where, aggregated, pre_grad):
    width = pre_grad.shape[1]
    return pl.pallas_call(
        weight_part_kernel,
        out_shape=(
            jax.ShapeDtypeStruct((128, width), F32),
            jax.ShapeDtypeStruct((128, width), BF16),
        ),
        in_specs=[pl.BlockSpec(memory_space=pltpu.SMEM)] + [WHOLE] * 2,
        out_specs=(WHOLE,) * 2,
        compiler_params=pltpu.CompilerParams(vmem_limit_bytes=SCOPED),
        name="weight_part",
    )(where, aggregated, pre_grad)


def weight_place_kernel(norm, where_ref, own_ref, core_ref, rep_ref, both_ref, out_ref):
    low, core = where_ref[0], where_ref[1]
    rows = own_ref.shape[0]
    for value, at_low, at_core in (
        (own_ref, low, core),
        (core_ref, low, 1 - core),
        (rep_ref, 1 - low, core),
        (both_ref, 1 - low, 1 - core),
    ):
        at = pl.multiple_of((at_low * 2 + at_core) * rows, rows)
        out_ref[pl.ds(at, rows), :] = value[...].astype(F32) * norm


def weight_place(where, blocks, norm):
    rows, width = blocks[0].shape
    return pl.pallas_call(
        lambda *refs: weight_place_kernel(norm, *refs),
        out_shape=jax.ShapeDtypeStruct((4 * rows, width), F32),
        in_specs=[pl.BlockSpec(memory_space=pltpu.SMEM)] + [WHOLE] * 4,
        out_specs=WHOLE,
        compiler_params=pltpu.CompilerParams(vmem_limit_bytes=SCOPED),
        name="weight_place",
    )(where, *blocks)


def swap_row(value, mask):
    return lax.ppermute(value, "row", [(r, r ^ mask) for r in range(16)])


def swap_core(value):
    return swap_row(value, 1)


def along_x(value, step):
    def target(r):
        return (r & 9) | ((((r >> 1) + step) & 3) << 1)

    return lax.ppermute(value, "row", [(r, target(r)) for r in range(16)])


def along_z(value, step):
    return lax.ppermute(value, "col", [(z, (z + step) % 8) for z in range(8)])


def swap_z(value, mask):
    return lax.ppermute(value, "col", [(z, z ^ mask) for z in range(8)])


def swap_rep(value):
    return lax.ppermute(value, "rep", [(0, 1), (1, 0)])


def swap_core_rep(value):
    pairs = [(2 * r + low, 2 * (r ^ 1) + 1 - low) for r in range(16) for low in range(2)]
    return lax.ppermute(value, ("row", "rep"), pairs)


LATE = ((1, 1), (3, 1), (2, 0), (2, 1))
SOON = ((0, 1), (1, 0), (3, 0))
ORDER = [(x, y, 1) for x, y in LATE] + [(x, y, 0) for x, y in LATE]
ORDER += [(x, y, 1) for x, y in SOON] + [(x, y, 0) for x, y in SOON]
ORDER += [(0, 0, 1), (0, 0, 0)]


def column_places(tile_columns):
    me = lax.axis_index("row")
    half, x, core = me >> 3, (me >> 1) & 3, me & 1
    dy = (tile_columns >> 3) ^ half
    dx = (((tile_columns >> 1) & 3) - x) & 3
    dc = (tile_columns & 1) ^ core
    key = dx * 4 + dy * 2 + dc
    place = jnp.zeros_like(key)
    for at, (bx, by, bc) in enumerate(ORDER):
        place = jnp.where(key == bx * 4 + by * 2 + bc, at, place)
    return place


def row_places(tile_rows):
    z, low = lax.axis_index("col"), lax.axis_index("rep")
    dz = ((tile_rows >> 1) - z) & 7
    return 2 * dz + ((tile_rows & 1) ^ low)


def body(features, tile_values, tile_coords, tile_counts, weight, cotangent):
    nodes = features.shape[0] * 256
    where = jnp.stack([lax.axis_index("rep"), lax.axis_index("row") & 1]).astype(jnp.int32)
    places = jnp.stack([row_places(tile_coords[:, 0]), column_places(tile_coords[:, 1])], -1)
    places = places.reshape(-1)

    half = swap_row(features, 8)
    left = along_x(features, 1)
    right = along_x(features, -1)
    core = swap_core(features)
    half, left, right, core, places, where = fence(half, left, right, core, places, where)
    sides = swap_row(stack(right, left), 8)
    far_half = swap_row(half, 4)
    far = along_x(left, 1)
    core_soon = swap_core(stack(half, right, left))
    dense = dense_block(tile_values, places, tile_counts)
    sides, far, far_half, core_soon, dense = fence(sides, far, far_half, core_soon, dense)
    late = stack(sides, far, far_half)
    core_late = swap_core(late)
    cot_twin = swap_rep(cotangent)
    pieces = (core_late, late, core_soon, half, right, left, core, features)

    middle = rows_dot(dense, pieces, (1024,), "rows_middle")
    up, down, middle = fence(middle[:128], middle[128:], middle)
    up, down = along_z(up, 1), along_z(down, -1)
    outer = rows_dot(dense, pieces, (768, 1280), "rows_outer")
    ahead, behind = outer[:256], outer[256:]
    up = stack(wide_sum(ahead[:128], up), ahead[128:])
    down = stack(behind[:128], wide_sum(behind[128:], down))
    up, down, cot_twin, core = fence(up, down, cot_twin, core)
    up, down = along_z(up, 1), along_z(down, -1)
    pieces = pieces[:6] + (core, features)
    inner = rows_dot(dense, pieces, (0, 256, 512, 1536, 1792), "rows_inner")

    def block(d):
        at = (0, 256, 512, 0, 0, 0, 768, 1024)[d]
        return inner[at : at + 256]

    up, down = fence(up, down)
    up, down = fence(wide_sum(block(2), up), wide_sum(block(6), down))
    up, down = along_z(up, 1), along_z(down, -1)
    up, down = fence(up, down)
    up, down = fence(wide_sum(block(1), up), wide_sum(block(7), down))
    up, down = along_z(up, 1), along_z(down, -1)
    mine = wide_sum(block(0), up, down)
    theirs = swap_rep(mine)
    aggregated, activations, pre_grad, here = layer(mine, theirs, weight, cotangent, cot_twin)

    here, aggregated, pre_grad = fence(here, aggregated, pre_grad)
    below, above = along_z(here, 1), along_z(here, -1)
    kept, sent = weight_part(where, aggregated, pre_grad)
    taken = swap_core(sent)
    near = below, above

    below, above, taken = fence(below, above, taken)
    share = wide_sum(kept, taken)
    below, above, share = fence(below, above, share)
    below, above = along_z(below, 1), along_z(above, -1)
    taken = [swap_row(share, 2 * m) for m in (1, 2, 3)]
    next_near = below, above

    below, above, *taken = fence(below, above, *taken)
    share = (share.astype(F32) + taken[0].astype(F32)) + (taken[1].astype(F32) + taken[2].astype(F32))
    share = share.astype(BF16)
    below, above, share = fence(below, above, share)
    below, above = along_z(below, 1), along_z(above, -1)
    taken = swap_row(share, 8)
    far = below, above

    below, above, taken = fence(below, above, taken)
    share = wide_sum(share, taken)
    below, above, share = fence(below[:256], above[256:], share)
    below, above = along_z(below, 1), along_z(above, -1)
    taken = swap_z(share, 1)
    below, above, taken = fence(below, above, taken)
    share = wide_sum(share, taken)
    rows = (here, near[1], next_near[1], far[1], below, above, far[0], next_near[0], near[0])

    other = columns_dot(dense, rows, 0, 4, "columns_other")
    other = swap_core(other)
    share = wide_sum(share, swap_z(share, 2))
    share = wide_sum(share, swap_z(share, 4))
    rest = columns_dot(dense, rows, 512, 12, "columns_rest")
    other, rest = fence(other, rest)
    late, soon, share = fence(wide_sum(rest[:4], other), rest[4:7], share)
    sides = swap_row(late[:2], 8)
    far_half = swap_row(late[3], 4)
    far = along_x(late[2], -1)
    soon = swap_core(soon)
    shares = share, swap_core(share), swap_rep(share), swap_core_rep(share)
    sides, far_half, far, soon, *shares = fence(sides, far_half, far, soon, *shares)
    half = wide_sum(rest[7], soon[0], far_half)
    right = wide_sum(rest[8], soon[1], sides[0])
    left = wide_sum(rest[9], soon[2], sides[1], far)
    half, right, left, core = fence(half, right, left, rest[10])
    half, right, left = swap_row(half, 8), along_x(right, 1), along_x(left, -1)
    core = swap_core(core)
    grad_weight = weight_place(where, shares, 1.0 / nodes**0.5)
    grad_features = finish(rest[11], half, right, left, core)
    return (activations, grad_features, grad_weight)


def solution(mesh):
    split = ("row", "col", "rep")
    placed = (P(split, None), P(split, None, None), P(split, None), P(split), P(), P(split, None))
    return jax.shard_map(
        body,
        mesh=mesh,
        in_specs=placed,
        out_specs=(P(split, None), P(split, None), P()),
        check_vma=False,
    )
```

```python
import jax
import jax.numpy as jnp
from jax import lax
from jax.experimental import pallas as pl
from jax.experimental.pallas import tpu as pltpu
from jax.sharding import PartitionSpec as P

TILE = 128
BUNCH = 16
SIDE = 2048
BLOCK = 256
F32 = jnp.float32
BF16 = jnp.bfloat16
MIB = 1024 * 1024
SCOPED = 8 * MIB
WHOLE = pl.BlockSpec(memory_space=pltpu.VMEM)


def wide_sum(*terms):
    total = terms[0].astype(F32)
    for term in terms[1:]:
        total = total + term.astype(F32)
    return total.astype(BF16)


def fence(*values):
    return lax.optimization_barrier(values)


def stack(*values):
    return jnp.concatenate(values, 0)


def dense_kernel(counts_ref, places_ref, tiles_ref, dense_ref, held_ref, arrived):
    bunches = held_ref.shape[0] // BUNCH

    def fetch(b):
        part = pl.ds(b * BUNCH, BUNCH)
        return pltpu.make_async_copy(tiles_ref.at[part], held_ref.at[part], arrived.at[b])

    for b in range(bunches):
        fetch(b).start()

    def clear(r, carry):
        dense_ref[pl.ds(pl.multiple_of(r * TILE, TILE), TILE), :] = jnp.zeros((TILE, SIDE), BF16)
        return carry

    lax.fori_loop(0, SIDE // TILE, clear, 0)
    live = counts_ref[0]
    for b in range(bunches):
        fetch(b).wait()

        def place(j, carry, b=b):
            slot = b * BUNCH + j

            @pl.when(slot < live)
            def _():
                top = pl.multiple_of(places_ref[2 * slot] * TILE, TILE)
                left = pl.multiple_of(places_ref[2 * slot + 1] * TILE, TILE)
                dense_ref[pl.ds(top, TILE), pl.ds(left, TILE)] = held_ref[slot]

            return carry

        lax.fori_loop(0, BUNCH, place, 0)


def dense_block(tile_values, places, tile_counts):
    slots = tile_values.shape[0]
    smem = pl.BlockSpec(memory_space=pltpu.SMEM)
    return pl.pallas_call(
        dense_kernel,
        out_shape=jax.ShapeDtypeStruct((SIDE, SIDE), BF16),
        in_specs=[smem, smem, pl.BlockSpec(memory_space=pltpu.HBM)],
        out_specs=WHOLE,
        scratch_shapes=[
            pltpu.VMEM(tile_values.shape, BF16),
            pltpu.SemaphoreType.DMA((slots // BUNCH,)),
        ],
        compiler_params=pltpu.CompilerParams(vmem_limit_bytes=SCOPED),
        cost_estimate=pl.CostEstimate(flops=0, bytes_accessed=12 * MIB, transcendentals=0),
        name="dense_build",
    )(tile_counts, places, tile_values)


def rows_kernel(first, dense_ref, *refs):
    pieces, (out_ref, panel_ref) = refs[:-2], refs[-2:]
    at = 0
    for piece in pieces:
        panel_ref[at : at + piece.shape[0], :] = piece[...]
        at += piece.shape[0]

    def product(i, carry):
        start = pl.multiple_of((first + i * BLOCK) & (SIDE - 1), BLOCK)
        out_ref[pl.ds(pl.multiple_of(i * BLOCK, BLOCK), BLOCK), :] = jnp.dot(
            dense_ref[pl.ds(start, BLOCK), :], panel_ref[...], preferred_element_type=F32
        ).astype(BF16)
        return carry

    lax.fori_loop(0, out_ref.shape[0] // BLOCK, product, 0)


def rows_dot(dense, pieces, first, rows, name):
    width = pieces[0].shape[1]
    return pl.pallas_call(
        lambda *refs: rows_kernel(first, *refs),
        out_shape=jax.ShapeDtypeStruct((rows, width), BF16),
        in_specs=[WHOLE] * (1 + len(pieces)),
        out_specs=WHOLE,
        scratch_shapes=[pltpu.VMEM((SIDE, width), BF16)],
        compiler_params=pltpu.CompilerParams(vmem_limit_bytes=SCOPED),
        cost_estimate=pl.CostEstimate(
            flops=2 * rows * SIDE * width, bytes_accessed=2 * rows * SIDE, transcendentals=0
        ),
        name=name,
    )(dense, *pieces)


def columns_kernel(first, dense_ref, *refs):
    pieces, (out_ref, panel_ref) = refs[:-2], refs[-2:]
    width = panel_ref.shape[0]
    down, across = 0, 0
    for piece in pieces:
        depth, step = piece.shape
        panel_ref[down : down + depth, across : across + step] = piece[...]
        down += depth
        if down == width:
            down, across = 0, across + step

    def product(i, carry):
        for j in range(2):
            begin = pl.multiple_of(first + (2 * i + j) * BLOCK, BLOCK)
            result = jnp.dot(
                panel_ref[...], dense_ref[:, pl.ds(begin, BLOCK)], preferred_element_type=F32
            ).astype(BF16)
            out_ref[4 * i + 2 * j] = result[:, :TILE]
            out_ref[4 * i + 2 * j + 1] = result[:, TILE:]
        return carry

    lax.fori_loop(0, out_ref.shape[0] // 4, product, 0)


def columns_dot(dense, pieces, first, blocks, name):
    width = pieces[0].shape[0]
    return pl.pallas_call(
        lambda *refs: columns_kernel(first, *refs),
        out_shape=jax.ShapeDtypeStruct((blocks, width, TILE), BF16),
        in_specs=[WHOLE] * (1 + len(pieces)),
        out_specs=WHOLE,
        scratch_shapes=[pltpu.VMEM((width, SIDE), BF16)],
        compiler_params=pltpu.CompilerParams(vmem_limit_bytes=SCOPED),
        cost_estimate=pl.CostEstimate(
            flops=2 * blocks * TILE * SIDE * width,
            bytes_accessed=2 * blocks * TILE * SIDE,
            transcendentals=0,
        ),
        name=name,
    )(dense, *pieces)


def layer_kernel(mine_ref, theirs_ref, weight_ref, cot_ref, twin_ref, agg_ref, act_ref, pre_grad_ref, grad_ref):
    half = cot_ref.shape[0]
    for at, cot in ((0, cot_ref), (half, twin_ref)):
        rows = slice(at, at + half)
        total = mine_ref[rows, :].astype(F32) + theirs_ref[half - at : 2 * half - at, :].astype(F32)
        aggregated = total.astype(BF16)
        agg_ref[rows, :] = aggregated
        pre_act = jnp.dot(aggregated, weight_ref[...], preferred_element_type=F32)
        gate = 1.0 / (1.0 + jnp.exp(-pre_act))
        if at == 0:
            act_ref[...] = (pre_act * gate).astype(BF16)
        slope = gate * (1.0 + pre_act * (1.0 - gate))
        pre_grad = (cot[...].astype(F32) * slope).astype(BF16)
        pre_grad_ref[rows, :] = pre_grad
        grad_ref[:, rows] = lax.dot_general(
            weight_ref[...], pre_grad, (((1,), (1,)), ((), ())), preferred_element_type=F32
        ).astype(BF16)


def layer(mine, theirs, weight, cotangent, cot_twin):
    rows, width = cotangent.shape
    both = jax.ShapeDtypeStruct((2 * rows, width), BF16)
    own = jax.ShapeDtypeStruct((rows, width), BF16)
    turned = jax.ShapeDtypeStruct((width, 2 * rows), BF16)
    return pl.pallas_call(
        layer_kernel,
        out_shape=(both, own, both, turned),
        in_specs=[WHOLE] * 5,
        out_specs=(WHOLE,) * 4,
        compiler_params=pltpu.CompilerParams(vmem_limit_bytes=SCOPED),
        name="layer",
    )(mine, theirs, weight, cotangent, cot_twin)


def finish_kernel(*refs):
    total = refs[0][...].astype(F32)
    for part in refs[1:-1]:
        total = total + part[...].astype(F32)
    refs[-1][...] = total.T.astype(BF16)


def finish(*parts):
    width, rows = parts[0].shape
    return pl.pallas_call(
        finish_kernel,
        out_shape=jax.ShapeDtypeStruct((rows, width), BF16),
        in_specs=[WHOLE] * len(parts),
        out_specs=WHOLE,
        compiler_params=pltpu.CompilerParams(vmem_limit_bytes=SCOPED),
        name="finish",
    )(*parts)


def weight_part_kernel(where_ref, agg_ref, pre_grad_ref, kept_ref, sent_ref):
    low, core = where_ref[0], where_ref[1]

    def rows_of(which):
        at = pl.multiple_of(low * 256 + which * 128, 128)
        return lax.dot_general(
            agg_ref[:, pl.ds(at, 128)],
            pre_grad_ref[...],
            (((0,), (0,)), ((), ())),
            preferred_element_type=F32,
        )

    kept_ref[...] = rows_of(core)
    sent_ref[...] = rows_of(1 - core).astype(BF16)


def weight_part(where, aggregated, pre_grad):
    width = pre_grad.shape[1]
    return pl.pallas_call(
        weight_part_kernel,
        out_shape=(
            jax.ShapeDtypeStruct((128, width), F32),
            jax.ShapeDtypeStruct((128, width), BF16),
        ),
        in_specs=[pl.BlockSpec(memory_space=pltpu.SMEM)] + [WHOLE] * 2,
        out_specs=(WHOLE,) * 2,
        compiler_params=pltpu.CompilerParams(vmem_limit_bytes=SCOPED),
        name="weight_part",
    )(where, aggregated, pre_grad)


def weight_place_kernel(norm, where_ref, own_ref, core_ref, rep_ref, both_ref, out_ref):
    low, core = where_ref[0], where_ref[1]
    rows = own_ref.shape[0]
    for value, at_low, at_core in (
        (own_ref, low, core),
        (core_ref, low, 1 - core),
        (rep_ref, 1 - low, core),
        (both_ref, 1 - low, 1 - core),
    ):
        at = pl.multiple_of((at_low * 2 + at_core) * rows, rows)
        out_ref[pl.ds(at, rows), :] = value[...].astype(F32) * norm


def weight_place(where, blocks, norm):
    rows, width = blocks[0].shape
    return pl.pallas_call(
        lambda *refs: weight_place_kernel(norm, *refs),
        out_shape=jax.ShapeDtypeStruct((4 * rows, width), F32),
        in_specs=[pl.BlockSpec(memory_space=pltpu.SMEM)] + [WHOLE] * 4,
        out_specs=WHOLE,
        compiler_params=pltpu.CompilerParams(vmem_limit_bytes=SCOPED),
        name="weight_place",
    )(where, *blocks)


def swap_row(value, mask):
    return lax.ppermute(value, "row", [(r, r ^ mask) for r in range(16)])


def swap_core(value):
    return swap_row(value, 1)


def along_x(value, step):
    def target(r):
        return (r & 9) | ((((r >> 1) + step) & 3) << 1)

    return lax.ppermute(value, "row", [(r, target(r)) for r in range(16)])


def along_z(value, step):
    return lax.ppermute(value, "col", [(z, (z + step) % 8) for z in range(8)])


def swap_z(value, mask):
    return lax.ppermute(value, "col", [(z, z ^ mask) for z in range(8)])


def swap_rep(value):
    return lax.ppermute(value, "rep", [(0, 1), (1, 0)])


def swap_core_rep(value):
    pairs = [(2 * r + low, 2 * (r ^ 1) + 1 - low) for r in range(16) for low in range(2)]
    return lax.ppermute(value, ("row", "rep"), pairs)


LATE = ((1, 1), (3, 1), (2, 0), (2, 1))
SOON = ((0, 1), (1, 0), (3, 0))
ORDER = [(x, y, 1) for x, y in LATE] + [(x, y, 0) for x, y in LATE]
ORDER += [(x, y, 1) for x, y in SOON] + [(x, y, 0) for x, y in SOON]
ORDER += [(0, 0, 1), (0, 0, 0)]


def column_places(tile_columns):
    me = lax.axis_index("row")
    half, x, core = me >> 3, (me >> 1) & 3, me & 1
    dy = (tile_columns >> 3) ^ half
    dx = (((tile_columns >> 1) & 3) - x) & 3
    dc = (tile_columns & 1) ^ core
    key = dx * 4 + dy * 2 + dc
    place = jnp.zeros_like(key)
    for at, (bx, by, bc) in enumerate(ORDER):
        place = jnp.where(key == bx * 4 + by * 2 + bc, at, place)
    return place


def row_places(tile_rows):
    z, low = lax.axis_index("col"), lax.axis_index("rep")
    dz = ((tile_rows >> 1) - z) & 7
    return 2 * dz + ((tile_rows & 1) ^ low)


def body(features, tile_values, tile_coords, tile_counts, weight, cotangent):
    nodes = features.shape[0] * 256
    where = jnp.stack([lax.axis_index("rep"), lax.axis_index("row") & 1]).astype(jnp.int32)
    places = jnp.stack([row_places(tile_coords[:, 0]), column_places(tile_coords[:, 1])], -1)
    places = places.reshape(-1)

    half = swap_row(features, 8)
    left = along_x(features, 1)
    right = along_x(features, -1)
    core = swap_core(features)
    half, left, right, core, places, where = fence(half, left, right, core, places, where)
    sides = swap_row(stack(right, left), 8)
    far_half = swap_row(half, 4)
    far = along_x(left, 1)
    core_soon = swap_core(stack(half, right, left))
    dense = dense_block(tile_values, places, tile_counts)
    sides, far, far_half, core_soon, dense = fence(sides, far, far_half, core_soon, dense)
    late = stack(sides, far, far_half)
    core_late = swap_core(late)
    cot_twin = swap_rep(cotangent)
    pieces = (core_late, late, core_soon, half, right, left, core, features)

    middle = rows_dot(dense, pieces, 1024, 256, "rows_middle")
    up, down, middle = fence(middle[:128], middle[128:], middle)
    up, down = along_z(up, 1), along_z(down, -1)
    rest = rows_dot(dense, pieces, 1280, 1792, "rows_rest")

    def block(d):
        at = (d - 5) % 8 * 256
        return rest[at : at + 256]

    ahead, behind = block(3), block(5)
    up = stack(wide_sum(ahead[:128], up), ahead[128:])
    down = stack(behind[:128], wide_sum(behind[128:], down))
    up, down, cot_twin = fence(up, down, cot_twin)
    up, down = along_z(up, 1), along_z(down, -1)
    up, down = fence(up, down)
    up, down = fence(wide_sum(block(2), up), wide_sum(block(6), down))
    up, down = along_z(up, 1), along_z(down, -1)
    up, down = fence(up, down)
    up, down = fence(wide_sum(block(1), up), wide_sum(block(7), down))
    up, down = along_z(up, 1), along_z(down, -1)
    mine = wide_sum(block(0), up, down)
    theirs = swap_rep(mine)
    aggregated, activations, pre_grad, here = layer(mine, theirs, weight, cotangent, cot_twin)

    here, aggregated, pre_grad = fence(here, aggregated, pre_grad)
    below, above = along_z(here, 1), along_z(here, -1)
    kept, sent = weight_part(where, aggregated, pre_grad)
    taken = swap_core(sent)
    near = below, above

    below, above, taken = fence(below, above, taken)
    share = wide_sum(kept, taken)
    below, above, share = fence(below, above, share)
    below, above = along_z(below, 1), along_z(above, -1)
    taken = [swap_row(share, 2 * m) for m in (1, 2, 3)]
    next_near = below, above

    below, above, *taken = fence(below, above, *taken)
    share = (share.astype(F32) + taken[0].astype(F32)) + (taken[1].astype(F32) + taken[2].astype(F32))
    share = share.astype(BF16)
    below, above, share = fence(below, above, share)
    below, above = along_z(below, 1), along_z(above, -1)
    taken = swap_row(share, 8)
    far = below, above

    below, above, taken = fence(below, above, taken)
    share = wide_sum(share, taken)
    below, above, share = fence(below[:256], above[256:], share)
    below, above = along_z(below, 1), along_z(above, -1)
    taken = swap_z(share, 1)
    below, above, taken = fence(below, above, taken)
    share = wide_sum(share, taken)
    rows = (here, near[1], next_near[1], far[1], below, above, far[0], next_near[0], near[0])

    other = columns_dot(dense, rows, 0, 4, "columns_other")
    other, share = fence(other, share)
    other = swap_core(other)
    taken = swap_z(share, 2)
    rest = columns_dot(dense, rows, 512, 12, "columns_rest")
    other, rest, taken = fence(other, rest, taken)
    late = wide_sum(rest[:4], other)
    share = wide_sum(share, taken)
    late, soon, share = fence(late, rest[4:7], share)
    sides = swap_row(late[:2], 8)
    far_half = swap_row(late[3], 4)
    far = along_x(late[2], -1)
    soon = swap_core(soon)
    taken = swap_z(share, 4)

    sides, far_half, far, soon, taken = fence(sides, far_half, far, soon, taken)
    half = wide_sum(rest[7], soon[0], far_half)
    right = wide_sum(rest[8], soon[1], sides[0])
    left = wide_sum(rest[9], soon[2], sides[1], far)
    share = wide_sum(share, taken)
    half, right, left, core, share = fence(half, right, left, rest[10], share)
    half, right, left = swap_row(half, 8), along_x(right, 1), along_x(left, -1)
    core = swap_core(core)
    shares = share, swap_core(share), swap_rep(share), swap_core_rep(share)
    grad_weight = weight_place(where, shares, 1.0 / nodes**0.5)
    grad_features = finish(rest[11], half, right, left, core)
    return (activations, grad_features, grad_weight)


def solution(mesh):
    split = ("row", "col", "rep")
    placed = (P(split, None), P(split, None, None), P(split, None), P(split), P(), P(split, None))
    return jax.shard_map(
        body,
        mesh=mesh,
        in_specs=placed,
        out_specs=(P(split, None), P(split, None), P()),
        check_vma=False,
    )
```

```python
import jax
import jax.numpy as jnp
from jax import lax
from jax.experimental import pallas as pl
from jax.experimental.pallas import tpu as pltpu
from jax.sharding import PartitionSpec as P

TILE = 128
BUNCH = 16
SIDE = 2048
BLOCK = 256
F32 = jnp.float32
BF16 = jnp.bfloat16
MIB = 1024 * 1024
SCOPED = 8 * MIB
WHOLE = pl.BlockSpec(memory_space=pltpu.VMEM)


def wide_sum(*terms):
    total = terms[0].astype(F32)
    for term in terms[1:]:
        total = total + term.astype(F32)
    return total.astype(BF16)


def fence(*values):
    return lax.optimization_barrier(values)


def stack(*values):
    return jnp.concatenate(values, 0)


def dense_kernel(counts_ref, places_ref, tiles_ref, dense_ref, held_ref, arrived):
    bunches = held_ref.shape[0] // BUNCH

    def fetch(b):
        part = pl.ds(b * BUNCH, BUNCH)
        return pltpu.make_async_copy(tiles_ref.at[part], held_ref.at[part], arrived.at[b])

    for b in range(bunches):
        fetch(b).start()

    def clear(r, carry):
        dense_ref[pl.ds(pl.multiple_of(r * TILE, TILE), TILE), :] = jnp.zeros((TILE, SIDE), BF16)
        return carry

    lax.fori_loop(0, SIDE // TILE, clear, 0)
    live = counts_ref[0]
    for b in range(bunches):
        fetch(b).wait()

        def place(j, carry, b=b):
            slot = b * BUNCH + j

            @pl.when(slot < live)
            def _():
                top = pl.multiple_of(places_ref[2 * slot] * TILE, TILE)
                left = pl.multiple_of(places_ref[2 * slot + 1] * TILE, TILE)
                dense_ref[pl.ds(top, TILE), pl.ds(left, TILE)] = held_ref[slot]

            return carry

        lax.fori_loop(0, BUNCH, place, 0)


def dense_block(tile_values, places, tile_counts):
    slots = tile_values.shape[0]
    smem = pl.BlockSpec(memory_space=pltpu.SMEM)
    return pl.pallas_call(
        dense_kernel,
        out_shape=jax.ShapeDtypeStruct((SIDE, SIDE), BF16),
        in_specs=[smem, smem, pl.BlockSpec(memory_space=pltpu.HBM)],
        out_specs=WHOLE,
        scratch_shapes=[
            pltpu.VMEM(tile_values.shape, BF16),
            pltpu.SemaphoreType.DMA((slots // BUNCH,)),
        ],
        compiler_params=pltpu.CompilerParams(vmem_limit_bytes=SCOPED),
        cost_estimate=pl.CostEstimate(flops=0, bytes_accessed=12 * MIB, transcendentals=0),
        name="dense_build",
    )(tile_counts, places, tile_values)


def rows_kernel(first, stride, dense_ref, *refs):
    pieces, (out_ref, panel_ref) = refs[:-2], refs[-2:]
    at = 0
    for piece in pieces:
        panel_ref[at : at + piece.shape[0], :] = piece[...]
        at += piece.shape[0]

    def product(i, carry):
        start = pl.multiple_of((first + i * stride) & (SIDE - 1), BLOCK)
        out_ref[pl.ds(pl.multiple_of(i * BLOCK, BLOCK), BLOCK), :] = jnp.dot(
            dense_ref[pl.ds(start, BLOCK), :], panel_ref[...], preferred_element_type=F32
        ).astype(BF16)
        return carry

    lax.fori_loop(0, out_ref.shape[0] // BLOCK, product, 0)


def rows_dot(dense, pieces, first, stride, rows, name):
    width = pieces[0].shape[1]
    return pl.pallas_call(
        lambda *refs: rows_kernel(first, stride, *refs),
        out_shape=jax.ShapeDtypeStruct((rows, width), BF16),
        in_specs=[WHOLE] * (1 + len(pieces)),
        out_specs=WHOLE,
        scratch_shapes=[pltpu.VMEM((SIDE, width), BF16)],
        compiler_params=pltpu.CompilerParams(vmem_limit_bytes=SCOPED),
        cost_estimate=pl.CostEstimate(
            flops=2 * rows * SIDE * width, bytes_accessed=2 * rows * SIDE, transcendentals=0
        ),
        name=name,
    )(dense, *pieces)


def columns_kernel(first, dense_ref, *refs):
    pieces, (out_ref, panel_ref) = refs[:-2], refs[-2:]
    width = panel_ref.shape[0]
    down, across = 0, 0
    for piece in pieces:
        depth, step = piece.shape
        panel_ref[down : down + depth, across : across + step] = piece[...]
        down += depth
        if down == width:
            down, across = 0, across + step

    def product(i, carry):
        for j in range(2):
            begin = pl.multiple_of(first + (2 * i + j) * BLOCK, BLOCK)
            result = jnp.dot(
                panel_ref[...], dense_ref[:, pl.ds(begin, BLOCK)], preferred_element_type=F32
            ).astype(BF16)
            out_ref[4 * i + 2 * j] = result[:, :TILE]
            out_ref[4 * i + 2 * j + 1] = result[:, TILE:]
        return carry

    lax.fori_loop(0, out_ref.shape[0] // 4, product, 0)


def columns_dot(dense, pieces, first, blocks, name):
    width = pieces[0].shape[0]
    return pl.pallas_call(
        lambda *refs: columns_kernel(first, *refs),
        out_shape=jax.ShapeDtypeStruct((blocks, width, TILE), BF16),
        in_specs=[WHOLE] * (1 + len(pieces)),
        out_specs=WHOLE,
        scratch_shapes=[pltpu.VMEM((width, SIDE), BF16)],
        compiler_params=pltpu.CompilerParams(vmem_limit_bytes=SCOPED),
        cost_estimate=pl.CostEstimate(
            flops=2 * blocks * TILE * SIDE * width,
            bytes_accessed=2 * blocks * TILE * SIDE,
            transcendentals=0,
        ),
        name=name,
    )(dense, *pieces)


def layer_kernel(mine_ref, theirs_ref, weight_ref, cot_ref, twin_ref, agg_ref, act_ref, pre_grad_ref, grad_ref):
    half = cot_ref.shape[0]
    for at, cot in ((0, cot_ref), (half, twin_ref)):
        rows = slice(at, at + half)
        total = mine_ref[rows, :].astype(F32) + theirs_ref[half - at : 2 * half - at, :].astype(F32)
        aggregated = total.astype(BF16)
        agg_ref[rows, :] = aggregated
        pre_act = jnp.dot(aggregated, weight_ref[...], preferred_element_type=F32)
        gate = 1.0 / (1.0 + jnp.exp(-pre_act))
        if at == 0:
            act_ref[...] = (pre_act * gate).astype(BF16)
        slope = gate * (1.0 + pre_act * (1.0 - gate))
        pre_grad = (cot[...].astype(F32) * slope).astype(BF16)
        pre_grad_ref[rows, :] = pre_grad
        grad_ref[:, rows] = lax.dot_general(
            weight_ref[...], pre_grad, (((1,), (1,)), ((), ())), preferred_element_type=F32
        ).astype(BF16)


def layer(mine, theirs, weight, cotangent, cot_twin):
    rows, width = cotangent.shape
    both = jax.ShapeDtypeStruct((2 * rows, width), BF16)
    own = jax.ShapeDtypeStruct((rows, width), BF16)
    turned = jax.ShapeDtypeStruct((width, 2 * rows), BF16)
    return pl.pallas_call(
        layer_kernel,
        out_shape=(both, own, both, turned),
        in_specs=[WHOLE] * 5,
        out_specs=(WHOLE,) * 4,
        compiler_params=pltpu.CompilerParams(vmem_limit_bytes=SCOPED),
        name="layer",
    )(mine, theirs, weight, cotangent, cot_twin)


def finish_kernel(*refs):
    total = refs[0][...].astype(F32)
    for part in refs[1:-1]:
        total = total + part[...].astype(F32)
    refs[-1][...] = total.T.astype(BF16)


def finish(*parts):
    width, rows = parts[0].shape
    return pl.pallas_call(
        finish_kernel,
        out_shape=jax.ShapeDtypeStruct((rows, width), BF16),
        in_specs=[WHOLE] * len(parts),
        out_specs=WHOLE,
        compiler_params=pltpu.CompilerParams(vmem_limit_bytes=SCOPED),
        name="finish",
    )(*parts)


def weight_part_kernel(where_ref, agg_ref, pre_grad_ref, kept_ref, sent_ref):
    low, core = where_ref[0], where_ref[1]

    def rows_of(which):
        at = pl.multiple_of(low * 256 + which * 128, 128)
        return lax.dot_general(
            agg_ref[:, pl.ds(at, 128)],
            pre_grad_ref[...],
            (((0,), (0,)), ((), ())),
            preferred_element_type=F32,
        )

    kept_ref[...] = rows_of(core)
    sent_ref[...] = rows_of(1 - core).astype(BF16)


def weight_part(where, aggregated, pre_grad):
    width = pre_grad.shape[1]
    return pl.pallas_call(
        weight_part_kernel,
        out_shape=(
            jax.ShapeDtypeStruct((128, width), F32),
            jax.ShapeDtypeStruct((128, width), BF16),
        ),
        in_specs=[pl.BlockSpec(memory_space=pltpu.SMEM)] + [WHOLE] * 2,
        out_specs=(WHOLE,) * 2,
        compiler_params=pltpu.CompilerParams(vmem_limit_bytes=SCOPED),
        name="weight_part",
    )(where, aggregated, pre_grad)


def weight_place_kernel(norm, where_ref, own_ref, core_ref, rep_ref, both_ref, out_ref):
    low, core = where_ref[0], where_ref[1]
    rows = own_ref.shape[0]
    for value, at_low, at_core in (
        (own_ref, low, core),
        (core_ref, low, 1 - core),
        (rep_ref, 1 - low, core),
        (both_ref, 1 - low, 1 - core),
    ):
        at = pl.multiple_of((at_low * 2 + at_core) * rows, rows)
        out_ref[pl.ds(at, rows), :] = value[...].astype(F32) * norm


def weight_place(where, blocks, norm):
    rows, width = blocks[0].shape
    return pl.pallas_call(
        lambda *refs: weight_place_kernel(norm, *refs),
        out_shape=jax.ShapeDtypeStruct((4 * rows, width), F32),
        in_specs=[pl.BlockSpec(memory_space=pltpu.SMEM)] + [WHOLE] * 4,
        out_specs=WHOLE,
        compiler_params=pltpu.CompilerParams(vmem_limit_bytes=SCOPED),
        name="weight_place",
    )(where, *blocks)


def swap_row(value, mask):
    return lax.ppermute(value, "row", [(r, r ^ mask) for r in range(16)])


def swap_core(value):
    return swap_row(value, 1)


def along_x(value, step):
    def target(r):
        return (r & 9) | ((((r >> 1) + step) & 3) << 1)

    return lax.ppermute(value, "row", [(r, target(r)) for r in range(16)])


def along_z(value, step):
    return lax.ppermute(value, "col", [(z, (z + step) % 8) for z in range(8)])


def swap_z(value, mask):
    return lax.ppermute(value, "col", [(z, z ^ mask) for z in range(8)])


def swap_rep(value):
    return lax.ppermute(value, "rep", [(0, 1), (1, 0)])


def swap_core_rep(value):
    pairs = [(2 * r + low, 2 * (r ^ 1) + 1 - low) for r in range(16) for low in range(2)]
    return lax.ppermute(value, ("row", "rep"), pairs)


LATE = ((1, 1), (3, 1), (2, 0), (2, 1))
SOON = ((0, 1), (1, 0), (3, 0))
ORDER = [(x, y, 1) for x, y in LATE] + [(x, y, 0) for x, y in LATE]
ORDER += [(x, y, 1) for x, y in SOON] + [(x, y, 0) for x, y in SOON]
ORDER += [(0, 0, 1), (0, 0, 0)]


def column_places(tile_columns):
    me = lax.axis_index("row")
    half, x, core = me >> 3, (me >> 1) & 3, me & 1
    dy = (tile_columns >> 3) ^ half
    dx = (((tile_columns >> 1) & 3) - x) & 3
    dc = (tile_columns & 1) ^ core
    key = dx * 4 + dy * 2 + dc
    place = jnp.zeros_like(key)
    for at, (bx, by, bc) in enumerate(ORDER):
        place = jnp.where(key == bx * 4 + by * 2 + bc, at, place)
    return place


def row_places(tile_rows):
    z, low = lax.axis_index("col"), lax.axis_index("rep")
    dz = ((tile_rows >> 1) - z) & 7
    return 2 * dz + ((tile_rows & 1) ^ low)


def body(features, tile_values, tile_coords, tile_counts, weight, cotangent):
    nodes = features.shape[0] * 256
    where = jnp.stack([lax.axis_index("rep"), lax.axis_index("row") & 1]).astype(jnp.int32)
    places = jnp.stack([row_places(tile_coords[:, 0]), column_places(tile_coords[:, 1])], -1)
    places = places.reshape(-1)

    half = swap_row(features, 8)
    left = along_x(features, 1)
    right = along_x(features, -1)
    core = swap_core(features)
    half, left, right, core, places, where = fence(half, left, right, core, places, where)
    sides = swap_row(stack(right, left), 8)
    far_half = swap_row(half, 4)
    far = along_x(left, 1)
    core_soon = swap_core(stack(half, right, left))
    dense = dense_block(tile_values, places, tile_counts)
    sides, far, far_half, core_soon, dense = fence(sides, far, far_half, core_soon, dense)
    late = stack(sides, far, far_half)
    core_late = swap_core(late)
    cot_twin = swap_rep(cotangent)
    pieces = (core_late, late, core_soon, half, right, left, core, features)

    middle = rows_dot(dense, pieces, 1024, 256, 256, "rows_middle")
    up, down, middle = fence(middle[:128], middle[128:], middle)
    up, down = along_z(up, 1), along_z(down, -1)
    outer = rows_dot(dense, pieces, 768, 512, 512, "rows_outer")
    ahead, behind = outer[:256], outer[256:]
    up = stack(wide_sum(ahead[:128], up), ahead[128:])
    down = stack(behind[:128], wide_sum(behind[128:], down))
    up, down, cot_twin, core = fence(up, down, cot_twin, core)
    up, down = along_z(up, 1), along_z(down, -1)
    inner = rows_dot(dense, pieces[:6] + (core, features), 1536, 256, 1280, "rows_inner")

    def block(d):
        at = (d - 6) % 8 * 256
        return inner[at : at + 256]

    up, down = fence(up, down)
    up, down = fence(wide_sum(block(2), up), wide_sum(block(6), down))
    up, down = along_z(up, 1), along_z(down, -1)
    up, down = fence(up, down)
    up, down = fence(wide_sum(block(1), up), wide_sum(block(7), down))
    up, down = along_z(up, 1), along_z(down, -1)
    mine = wide_sum(block(0), up, down)
    theirs = swap_rep(mine)
    aggregated, activations, pre_grad, here = layer(mine, theirs, weight, cotangent, cot_twin)

    here, aggregated, pre_grad = fence(here, aggregated, pre_grad)
    below, above = along_z(here, 1), along_z(here, -1)
    kept, sent = weight_part(where, aggregated, pre_grad)
    taken = swap_core(sent)
    near = below, above

    below, above, taken = fence(below, above, taken)
    share = wide_sum(kept, taken)
    below, above, share = fence(below, above, share)
    below, above = along_z(below, 1), along_z(above, -1)
    taken = [swap_row(share, 2 * m) for m in (1, 2, 3)]
    next_near = below, above

    below, above, *taken = fence(below, above, *taken)
    share = (share.astype(F32) + taken[0].astype(F32)) + (taken[1].astype(F32) + taken[2].astype(F32))
    share = share.astype(BF16)
    below, above, share = fence(below, above, share)
    below, above = along_z(below, 1), along_z(above, -1)
    taken = swap_row(share, 8)
    far = below, above

    below, above, taken = fence(below, above, taken)
    share = wide_sum(share, taken)
    below, above, share = fence(below[:256], above[256:], share)
    below, above = along_z(below, 1), along_z(above, -1)
    taken = swap_z(share, 1)
    below, above, taken = fence(below, above, taken)
    share = wide_sum(share, taken)
    rows = (here, near[1], next_near[1], far[1], below, above, far[0], next_near[0], near[0])

    other = columns_dot(dense, rows, 0, 4, "columns_other")
    other = swap_core(other)
    taken = swap_z(share, 2)
    rest = columns_dot(dense, rows, 512, 12, "columns_rest")
    other, rest, taken = fence(other, rest, taken)
    late = wide_sum(rest[:4], other)
    share = wide_sum(share, taken)
    late, soon, share = fence(late, rest[4:7], share)
    sides = swap_row(late[:2], 8)
    far_half = swap_row(late[3], 4)
    far = along_x(late[2], -1)
    soon = swap_core(soon)
    taken = swap_z(share, 4)

    sides, far_half, far, soon, taken = fence(sides, far_half, far, soon, taken)
    half = wide_sum(rest[7], soon[0], far_half)
    right = wide_sum(rest[8], soon[1], sides[0])
    left = wide_sum(rest[9], soon[2], sides[1], far)
    share = wide_sum(share, taken)
    half, right, left, core, share = fence(half, right, left, rest[10], share)
    half, right, left = swap_row(half, 8), along_x(right, 1), along_x(left, -1)
    core = swap_core(core)
    shares = share, swap_core(share), swap_rep(share), swap_core_rep(share)
    grad_weight = weight_place(where, shares, 1.0 / nodes**0.5)
    grad_features = finish(rest[11], half, right, left, core)
    return (activations, grad_features, grad_weight)


def solution(mesh):
    split = ("row", "col", "rep")
    placed = (P(split, None), P(split, None, None), P(split, None), P(split), P(), P(split, None))
    return jax.shard_map(
        body,
        mesh=mesh,
        in_specs=placed,
        out_specs=(P(split, None), P(split, None), P()),
        check_vma=False,
    )
```

```python
import jax
import jax.numpy as jnp
from jax import lax
from jax.experimental import pallas as pl
from jax.experimental.pallas import tpu as pltpu
from jax.sharding import PartitionSpec as P

TILE = 128
SIDE = 2048
BLOCK = 256
F32 = jnp.float32
BF16 = jnp.bfloat16
MIB = 1024 * 1024
SCOPED = 8 * MIB
WHOLE = pl.BlockSpec(memory_space=pltpu.VMEM)


def wide_sum(*terms):
    total = terms[0].astype(F32)
    for term in terms[1:]:
        total = total + term.astype(F32)
    return total.astype(BF16)


def fence(*values):
    return lax.optimization_barrier(values)


def stack(*values):
    return jnp.concatenate(values, 0)


def dense_kernel(counts_ref, places_ref, tiles_ref, dense_ref):
    def clear(r, carry):
        dense_ref[pl.ds(pl.multiple_of(r * TILE, TILE), TILE), :] = jnp.zeros((TILE, SIDE), BF16)
        return carry

    lax.fori_loop(0, SIDE // TILE, clear, 0)

    def place(slot, carry):
        top = pl.multiple_of(places_ref[2 * slot] * TILE, TILE)
        left = pl.multiple_of(places_ref[2 * slot + 1] * TILE, TILE)
        dense_ref[pl.ds(top, TILE), pl.ds(left, TILE)] = tiles_ref[slot]
        return carry

    lax.fori_loop(0, counts_ref[0], place, 0)


def dense_block(tile_values, places, tile_counts):
    smem = pl.BlockSpec(memory_space=pltpu.SMEM)
    return pl.pallas_call(
        dense_kernel,
        out_shape=jax.ShapeDtypeStruct((SIDE, SIDE), BF16),
        in_specs=[smem, smem, WHOLE],
        out_specs=WHOLE,
        compiler_params=pltpu.CompilerParams(vmem_limit_bytes=SCOPED),
        cost_estimate=pl.CostEstimate(flops=0, bytes_accessed=12 * MIB, transcendentals=0),
        name="dense_build",
    )(tile_counts, places, tile_values)


def rows_kernel(first, stride, dense_ref, *refs):
    pieces, (out_ref, panel_ref) = refs[:-2], refs[-2:]
    at = 0
    for piece in pieces:
        panel_ref[at : at + piece.shape[0], :] = piece[...]
        at += piece.shape[0]

    def product(i, carry):
        start = pl.multiple_of((first + i * stride) & (SIDE - 1), BLOCK)
        out_ref[pl.ds(pl.multiple_of(i * BLOCK, BLOCK), BLOCK), :] = jnp.dot(
            dense_ref[pl.ds(start, BLOCK), :], panel_ref[...], preferred_element_type=F32
        ).astype(BF16)
        return carry

    lax.fori_loop(0, out_ref.shape[0] // BLOCK, product, 0)


def rows_dot(dense, pieces, first, stride, rows, name):
    width = pieces[0].shape[1]
    return pl.pallas_call(
        lambda *refs: rows_kernel(first, stride, *refs),
        out_shape=jax.ShapeDtypeStruct((rows, width), BF16),
        in_specs=[WHOLE] * (1 + len(pieces)),
        out_specs=WHOLE,
        scratch_shapes=[pltpu.VMEM((SIDE, width), BF16)],
        compiler_params=pltpu.CompilerParams(vmem_limit_bytes=SCOPED),
        cost_estimate=pl.CostEstimate(
            flops=2 * rows * SIDE * width, bytes_accessed=2 * rows * SIDE, transcendentals=0
        ),
        name=name,
    )(dense, *pieces)


def columns_kernel(first, dense_ref, *refs):
    pieces, (out_ref, panel_ref) = refs[:-2], refs[-2:]
    width = panel_ref.shape[0]
    down, across = 0, 0
    for piece in pieces:
        depth, step = piece.shape
        panel_ref[down : down + depth, across : across + step] = piece[...]
        down += depth
        if down == width:
            down, across = 0, across + step

    def product(i, carry):
        for j in range(2):
            begin = pl.multiple_of(first + (2 * i + j) * BLOCK, BLOCK)
            result = jnp.dot(
                panel_ref[...], dense_ref[:, pl.ds(begin, BLOCK)], preferred_element_type=F32
            ).astype(BF16)
            out_ref[4 * i + 2 * j] = result[:, :TILE]
            out_ref[4 * i + 2 * j + 1] = result[:, TILE:]
        return carry

    lax.fori_loop(0, out_ref.shape[0] // 4, product, 0)


def columns_dot(dense, pieces, first, blocks, name):
    width = pieces[0].shape[0]
    return pl.pallas_call(
        lambda *refs: columns_kernel(first, *refs),
        out_shape=jax.ShapeDtypeStruct((blocks, width, TILE), BF16),
        in_specs=[WHOLE] * (1 + len(pieces)),
        out_specs=WHOLE,
        scratch_shapes=[pltpu.VMEM((width, SIDE), BF16)],
        compiler_params=pltpu.CompilerParams(vmem_limit_bytes=SCOPED),
        cost_estimate=pl.CostEstimate(
            flops=2 * blocks * TILE * SIDE * width,
            bytes_accessed=2 * blocks * TILE * SIDE,
            transcendentals=0,
        ),
        name=name,
    )(dense, *pieces)


def layer_kernel(mine_ref, theirs_ref, weight_ref, cot_ref, twin_ref, agg_ref, act_ref, pre_grad_ref, grad_ref):
    half = cot_ref.shape[0]
    for at, cot in ((0, cot_ref), (half, twin_ref)):
        rows = slice(at, at + half)
        total = mine_ref[rows, :].astype(F32) + theirs_ref[half - at : 2 * half - at, :].astype(F32)
        aggregated = total.astype(BF16)
        agg_ref[rows, :] = aggregated
        pre_act = jnp.dot(aggregated, weight_ref[...], preferred_element_type=F32)
        gate = 1.0 / (1.0 + jnp.exp(-pre_act))
        if at == 0:
            act_ref[...] = (pre_act * gate).astype(BF16)
        slope = gate * (1.0 + pre_act * (1.0 - gate))
        pre_grad = (cot[...].astype(F32) * slope).astype(BF16)
        pre_grad_ref[rows, :] = pre_grad
        grad_ref[:, rows] = lax.dot_general(
            weight_ref[...], pre_grad, (((1,), (1,)), ((), ())), preferred_element_type=F32
        ).astype(BF16)


def layer(mine, theirs, weight, cotangent, cot_twin):
    rows, width = cotangent.shape
    both = jax.ShapeDtypeStruct((2 * rows, width), BF16)
    own = jax.ShapeDtypeStruct((rows, width), BF16)
    turned = jax.ShapeDtypeStruct((width, 2 * rows), BF16)
    return pl.pallas_call(
        layer_kernel,
        out_shape=(both, own, both, turned),
        in_specs=[WHOLE] * 5,
        out_specs=(WHOLE,) * 4,
        compiler_params=pltpu.CompilerParams(vmem_limit_bytes=SCOPED),
        name="layer",
    )(mine, theirs, weight, cotangent, cot_twin)


def finish_kernel(*refs):
    total = refs[0][...].astype(F32)
    for part in refs[1:-1]:
        total = total + part[...].astype(F32)
    refs[-1][...] = total.T.astype(BF16)


def finish(*parts):
    width, rows = parts[0].shape
    return pl.pallas_call(
        finish_kernel,
        out_shape=jax.ShapeDtypeStruct((rows, width), BF16),
        in_specs=[WHOLE] * len(parts),
        out_specs=WHOLE,
        compiler_params=pltpu.CompilerParams(vmem_limit_bytes=SCOPED),
        name="finish",
    )(*parts)


def weight_part_kernel(where_ref, agg_ref, pre_grad_ref, kept_ref, sent_ref):
    low, core = where_ref[0], where_ref[1]

    def rows_of(which):
        at = pl.multiple_of(low * 256 + which * 128, 128)
        return lax.dot_general(
            agg_ref[:, pl.ds(at, 128)],
            pre_grad_ref[...],
            (((0,), (0,)), ((), ())),
            preferred_element_type=F32,
        )

    kept_ref[...] = rows_of(core)
    sent_ref[...] = rows_of(1 - core).astype(BF16)


def weight_part(where, aggregated, pre_grad):
    width = pre_grad.shape[1]
    return pl.pallas_call(
        weight_part_kernel,
        out_shape=(
            jax.ShapeDtypeStruct((128, width), F32),
            jax.ShapeDtypeStruct((128, width), BF16),
        ),
        in_specs=[pl.BlockSpec(memory_space=pltpu.SMEM)] + [WHOLE] * 2,
        out_specs=(WHOLE,) * 2,
        compiler_params=pltpu.CompilerParams(vmem_limit_bytes=SCOPED),
        name="weight_part",
    )(where, aggregated, pre_grad)


def weight_place_kernel(norm, where_ref, own_ref, core_ref, rep_ref, both_ref, out_ref):
    low, core = where_ref[0], where_ref[1]
    rows = own_ref.shape[0]
    for value, at_low, at_core in (
        (own_ref, low, core),
        (core_ref, low, 1 - core),
        (rep_ref, 1 - low, core),
        (both_ref, 1 - low, 1 - core),
    ):
        at = pl.multiple_of((at_low * 2 + at_core) * rows, rows)
        out_ref[pl.ds(at, rows), :] = value[...].astype(F32) * norm


def weight_place(where, blocks, norm):
    rows, width = blocks[0].shape
    return pl.pallas_call(
        lambda *refs: weight_place_kernel(norm, *refs),
        out_shape=jax.ShapeDtypeStruct((4 * rows, width), F32),
        in_specs=[pl.BlockSpec(memory_space=pltpu.SMEM)] + [WHOLE] * 4,
        out_specs=WHOLE,
        compiler_params=pltpu.CompilerParams(vmem_limit_bytes=SCOPED),
        name="weight_place",
    )(where, *blocks)


def swap_row(value, mask):
    return lax.ppermute(value, "row", [(r, r ^ mask) for r in range(16)])


def swap_core(value):
    return swap_row(value, 1)


def along_x(value, step):
    def target(r):
        return (r & 9) | ((((r >> 1) + step) & 3) << 1)

    return lax.ppermute(value, "row", [(r, target(r)) for r in range(16)])


def along_z(value, step):
    return lax.ppermute(value, "col", [(z, (z + step) % 8) for z in range(8)])


def swap_z(value, mask):
    return lax.ppermute(value, "col", [(z, z ^ mask) for z in range(8)])


def swap_rep(value):
    return lax.ppermute(value, "rep", [(0, 1), (1, 0)])


def swap_core_rep(value):
    pairs = [(2 * r + low, 2 * (r ^ 1) + 1 - low) for r in range(16) for low in range(2)]
    return lax.ppermute(value, ("row", "rep"), pairs)


LATE = ((1, 1), (3, 1), (2, 0), (2, 1))
SOON = ((0, 1), (1, 0), (3, 0))
ORDER = [(x, y, 1) for x, y in LATE] + [(x, y, 0) for x, y in LATE]
ORDER += [(x, y, 1) for x, y in SOON] + [(x, y, 0) for x, y in SOON]
ORDER += [(0, 0, 1), (0, 0, 0)]


def column_places(tile_columns):
    me = lax.axis_index("row")
    half, x, core = me >> 3, (me >> 1) & 3, me & 1
    dy = (tile_columns >> 3) ^ half
    dx = (((tile_columns >> 1) & 3) - x) & 3
    dc = (tile_columns & 1) ^ core
    key = dx * 4 + dy * 2 + dc
    place = jnp.zeros_like(key)
    for at, (bx, by, bc) in enumerate(ORDER):
        place = jnp.where(key == bx * 4 + by * 2 + bc, at, place)
    return place


def row_places(tile_rows):
    z, low = lax.axis_index("col"), lax.axis_index("rep")
    dz = ((tile_rows >> 1) - z) & 7
    return 2 * dz + ((tile_rows & 1) ^ low)


def body(features, tile_values, tile_coords, tile_counts, weight, cotangent):
    nodes = features.shape[0] * 256
    where = jnp.stack([lax.axis_index("rep"), lax.axis_index("row") & 1]).astype(jnp.int32)
    places = jnp.stack([row_places(tile_coords[:, 0]), column_places(tile_coords[:, 1])], -1)
    places = places.reshape(-1)

    half = swap_row(features, 8)
    left = along_x(features, 1)
    right = along_x(features, -1)
    core = swap_core(features)
    half, left, right, core, places, where = fence(half, left, right, core, places, where)
    sides = swap_row(stack(right, left), 8)
    far_half = swap_row(half, 4)
    far = along_x(left, 1)
    core_soon = swap_core(stack(half, right, left))
    dense = dense_block(tile_values, places, tile_counts)
    sides, far, far_half, core_soon, dense = fence(sides, far, far_half, core_soon, dense)
    late = stack(sides, far, far_half)
    core_late = swap_core(late)
    cot_twin = swap_rep(cotangent)
    pieces = (core_late, late, core_soon, half, right, left, core, features)

    middle = rows_dot(dense, pieces, 1024, 256, 256, "rows_middle")
    up, down, middle = fence(middle[:128], middle[128:], middle)
    up, down = along_z(up, 1), along_z(down, -1)
    outer = rows_dot(dense, pieces, 768, 512, 512, "rows_outer")
    ahead, behind = outer[:256], outer[256:]
    up = stack(wide_sum(ahead[:128], up), ahead[128:])
    down = stack(behind[:128], wide_sum(behind[128:], down))
    up, down, cot_twin, core = fence(up, down, cot_twin, core)
    up, down = along_z(up, 1), along_z(down, -1)
    inner = rows_dot(dense, pieces[:6] + (core, features), 1536, 256, 1280, "rows_inner")

    def block(d):
        at = (d - 6) % 8 * 256
        return inner[at : at + 256]

    up, down = fence(up, down)
    up, down = fence(wide_sum(block(2), up), wide_sum(block(6), down))
    up, down = along_z(up, 1), along_z(down, -1)
    up, down = fence(up, down)
    up, down = fence(wide_sum(block(1), up), wide_sum(block(7), down))
    up, down = along_z(up, 1), along_z(down, -1)
    mine = wide_sum(block(0), up, down)
    theirs = swap_rep(mine)
    aggregated, activations, pre_grad, here = layer(mine, theirs, weight, cotangent, cot_twin)

    here, aggregated, pre_grad = fence(here, aggregated, pre_grad)
    below, above = along_z(here, 1), along_z(here, -1)
    kept, sent = weight_part(where, aggregated, pre_grad)
    taken = swap_core(sent)
    near = below, above

    below, above, taken = fence(below, above, taken)
    share = wide_sum(kept, taken)
    below, above, share = fence(below, above, share)
    below, above = along_z(below, 1), along_z(above, -1)
    taken = [swap_row(share, 2 * m) for m in (1, 2, 3)]
    next_near = below, above

    below, above, *taken = fence(below, above, *taken)
    share = (share.astype(F32) + taken[0].astype(F32)) + (taken[1].astype(F32) + taken[2].astype(F32))
    share = share.astype(BF16)
    below, above, share = fence(below, above, share)
    below, above = along_z(below, 1), along_z(above, -1)
    taken = swap_row(share, 8)
    far = below, above

    below, above, taken = fence(below, above, taken)
    share = wide_sum(share, taken)
    below, above, share = fence(below[:256], above[256:], share)
    below, above = along_z(below, 1), along_z(above, -1)
    taken = swap_z(share, 1)
    below, above, taken = fence(below, above, taken)
    share = wide_sum(share, taken)
    rows = (here, near[1], next_near[1], far[1], below, above, far[0], next_near[0], near[0])

    other = columns_dot(dense, rows, 0, 4, "columns_other")
    other = swap_core(other)
    taken = swap_z(share, 2)
    rest = columns_dot(dense, rows, 512, 12, "columns_rest")
    other, rest, taken = fence(other, rest, taken)
    late = wide_sum(rest[:4], other)
    share = wide_sum(share, taken)
    late, soon, share = fence(late, rest[4:7], share)
    sides = swap_row(late[:2], 8)
    far_half = swap_row(late[3], 4)
    far = along_x(late[2], -1)
    soon = swap_core(soon)
    taken = swap_z(share, 4)

    sides, far_half, far, soon, taken = fence(sides, far_half, far, soon, taken)
    half = wide_sum(rest[7], soon[0], far_half)
    right = wide_sum(rest[8], soon[1], sides[0])
    left = wide_sum(rest[9], soon[2], sides[1], far)
    share = wide_sum(share, taken)
    half, right, left, core, share = fence(half, right, left, rest[10], share)
    half, right, left = swap_row(half, 8), along_x(right, 1), along_x(left, -1)
    core = swap_core(core)
    shares = share, swap_core(share), swap_rep(share), swap_core_rep(share)
    grad_weight = weight_place(where, shares, 1.0 / nodes**0.5)
    grad_features = finish(rest[11], half, right, left, core)
    return (activations, grad_features, grad_weight)


def solution(mesh):
    split = ("row", "col", "rep")
    placed = (P(split, None), P(split, None, None), P(split, None), P(split), P(), P(split, None))
    return jax.shard_map(
        body,
        mesh=mesh,
        in_specs=placed,
        out_specs=(P(split, None), P(split, None), P()),
        check_vma=False,
    )
```
